32 devices in a mesh: row: 4 (over y, x), col: 8 (over z, core).
Axes of the slice: x: 2, y: 2, z: 4, core: 2. Of those that a mesh axis runs over, the one named last changes fastest.
Arguments:
- block_values: float32 [4, 8, 40, 128, 128], P('row', 'col'), may hold values from 7.8125e-06 to 0.00078125
- block_index: int32 [4, 8, 2, 40], P('row', 'col'), may hold values from 0 to 15, as said below
- block_count: int32 [4, 8], P('row', 'col'), may hold values from 1 to 40, as said below
- strength: float32 [32], replicated, may hold values from 1 to 30
- raw_scores: float32 [64, 32, 128], P(('row', 'col')), may hold values from -24 to 24
Outputs:
- smoothed: float32 [64, 32, 128], P(('row', 'col'))
- final_residual: float32 [64, 32, 128], P(('row', 'col'))
The draws below stay inside these ranges and needn't reach their ends.
Inputs may be any that keep to these rules, and one draw needn't show every extreme that they name: `block_count`: some device has exactly 40 live slots; the others hold between half and all of their share of the upper triangle, scaled to 40. `block_index`: the live slots of one device name distinct blocks, each with global block row at most its global block column; slots at or above the count hold pairs in range that are ignored.
All inputs are finite; a program needn't handle non-finite values.
Results may differ from the reference program's by a relative error of at most 0.0003.
Values sent between devices are 32-bit elements; how exact they have to be, the bound alone decides.
No kernel may reach another device: no remote copies, remote signals or barrier semaphores. Data moves between devices by JAX's collectives and lax.ppermute only.
A program may use at most 64 MiB of HBM per device.

```python
import math
import jax
import jax.numpy as jnp
from jax import lax

BS = 128
RHS = 32
SEG = 2
ITERS = 3
CAP = 40
NB = 64
N_ROW = 4
N_COL = 8


def block_pattern(key):
    rows_here = N_COL * SEG
    cols_here = N_ROW * SEG
    row_ids = jnp.arange(N_ROW, dtype=jnp.int32)[:, None, None, None]
    col_ids = jnp.arange(N_COL, dtype=jnp.int32)[None, :, None, None]
    local_rows = jnp.arange(rows_here, dtype=jnp.int32)[None, None, :, None]
    local_cols = jnp.arange(cols_here, dtype=jnp.int32)[None, None, None, :]
    global_rows = row_ids * rows_here + local_rows
    global_cols = (local_cols // SEG * N_COL + col_ids) * SEG + local_cols % SEG
    valid = (global_rows <= global_cols).astype(jnp.int32)
    valid_count = jnp.sum(valid, axis=(2, 3))
    top_count = jnp.max(valid_count)
    share_count = jnp.maximum(1, CAP * valid_count // top_count)
    cut = jax.random.randint(jax.random.fold_in(key, 13), (N_ROW, N_COL), 0, share_count // 2 + 1, dtype=jnp.int32)
    live_count = jnp.clip(share_count - cut, 1, CAP)
    flat_pos = jnp.arange(N_ROW * N_COL, dtype=jnp.int32).reshape(N_ROW, N_COL)
    busiest = jnp.argmax(valid_count.reshape(-1)).astype(jnp.int32)
    live_count = jnp.where(flat_pos == busiest, CAP, live_count)
    cells = rows_here * cols_here
    flat_valid = valid.reshape(N_ROW, N_COL, cells)
    split_keys = jax.random.split(jax.random.fold_in(key, 11), N_ROW * N_COL)
    shuffled = jax.vmap(lambda one_key: jax.random.permutation(one_key, cells))(split_keys).reshape(N_ROW, N_COL, cells).astype(jnp.int32)
    flat_index = jnp.arange(cells, dtype=jnp.int32)[None, None, :]
    scores = jnp.where(flat_valid > 0, shuffled + 1, -(flat_index + 1))
    _, chosen = lax.top_k(scores, CAP)
    chosen = chosen.astype(jnp.int32)
    index_pairs = jnp.stack([chosen // cols_here, chosen % cols_here], axis=2)
    return (index_pairs, live_count.astype(jnp.int32))


def draw_block_index(key, part):
    index_pairs, live_count = block_pattern(jax.random.fold_in(key, 5))
    return index_pairs


def draw_block_count(key, part):
    index_pairs, live_count = block_pattern(jax.random.fold_in(key, 5))
    return live_count


def draw_raw_scores(key, part):
    ramp = (3.0 ** (jnp.arange(NB, dtype=jnp.float32) / NB))[:, None, None]
    base = jnp.clip(jax.random.normal(jax.random.fold_in(key, 23), (NB, RHS, BS), jnp.float32), -6.0, 6.0)
    return base * ramp


def block_levels(own_key, dims, cuts, smallest, largest):
    def one(dim, parts):
        steps = jax.random.uniform(jax.random.fold_in(jax.random.fold_in(own_key, 6), dim), (parts,), jnp.float32, smallest / len(cuts), largest / len(cuts))
        return jnp.repeat(jnp.exp(steps), dims[dim] // parts).reshape((-1,) + (1,) * (len(dims) - dim - 1))

    factor_of = one(*cuts[0])
    for cut in cuts[1:]:
        factor_of = factor_of * one(*cut)
    return factor_of


def setup_inputs(seed: int = 0) -> dict:
    splits = jax.random.split(jax.random.key(seed), 6)
    return {
        "block_values": jnp.clip(jnp.exp(math.log(0.00078125) - 4.6051702 * jax.random.uniform(splits[0], (N_ROW, N_COL, CAP, BS, BS), jnp.float32) ** block_levels(splits[0], (N_ROW, N_COL, CAP, BS, BS), ((0, 4), (1, 8)), -0.2, 0.2)), 7.812500371073838e-06, 0.00078125),
        "block_index": draw_block_index(jax.random.fold_in(splits[5], 71), 0),
        "block_count": draw_block_count(jax.random.fold_in(splits[5], 71), 0),
        "strength": jnp.clip(jnp.exp(jax.random.uniform(splits[3], (RHS,), jnp.float32, math.log(1.0), math.log(30.0))), 1.0, 30.0),
        "raw_scores": draw_raw_scores(jax.random.fold_in(splits[5], 71), 0),
    }


def local_terms(values, row_index, col_index, panel_rows, panel_cols):
    picked_cols = jnp.take(panel_cols, col_index, axis=0)
    picked_rows = jnp.take(panel_rows, row_index, axis=0)
    to_rows = jnp.einsum("crk,cik->cri", picked_cols, values, precision=lax.Precision.HIGHEST)
    to_cols = jnp.einsum("cri,cik->crk", picked_rows, values, precision=lax.Precision.HIGHEST)
    row_part = jax.ops.segment_sum(to_rows, row_index, num_segments=panel_rows.shape[0])
    col_part = jax.ops.segment_sum(to_cols, col_index, num_segments=panel_cols.shape[0])
    return row_part, col_part


def apply_graph(vector, block_values, block_index, block_count):
    width = vector.shape[1]
    panel_grid = vector.reshape(N_ROW, N_COL, SEG, width, BS)

    def device_step(total_sum, device):
        row_pos = device // N_COL
        col_pos = device % N_COL
        panel_rows = lax.dynamic_index_in_dim(panel_grid, row_pos, 0, keepdims=False).reshape(N_COL * SEG, width, BS)
        panel_cols = lax.dynamic_index_in_dim(panel_grid, col_pos, 1, keepdims=False).reshape(N_ROW * SEG, width, BS)
        device_values = lax.dynamic_index_in_dim(lax.dynamic_index_in_dim(block_values, row_pos, 0, keepdims=False), col_pos, 0, keepdims=False)
        device_index = lax.dynamic_index_in_dim(lax.dynamic_index_in_dim(block_index, row_pos, 0, keepdims=False), col_pos, 0, keepdims=False)
        device_count = lax.dynamic_index_in_dim(lax.dynamic_index_in_dim(block_count, row_pos, 0, keepdims=False), col_pos, 0, keepdims=False)
        live_mask = (jnp.arange(CAP, dtype=jnp.int32) < device_count.astype(jnp.int32)).astype(jnp.float32)
        masked = device_values * live_mask[:, None, None]
        row_part, col_part = local_terms(masked, device_index[0].astype(jnp.int32), device_index[1].astype(jnp.int32), panel_rows, panel_cols)
        row_slab = lax.dynamic_index_in_dim(total_sum, row_pos, 0, keepdims=False) + row_part.reshape(N_COL, SEG, width, BS)
        total_sum = lax.dynamic_update_index_in_dim(total_sum, row_slab, row_pos, 0)
        col_slab = lax.dynamic_index_in_dim(total_sum, col_pos, 1, keepdims=False) + col_part.reshape(N_ROW, SEG, width, BS)
        total_sum = lax.dynamic_update_index_in_dim(total_sum, col_slab, col_pos, 1)
        return total_sum, None

    start = jnp.zeros((N_ROW, N_COL, SEG, width, BS), jnp.float32)
    total_sum, _ = lax.scan(device_step, start, jnp.arange(N_ROW * N_COL, dtype=jnp.int32))
    return total_sum.reshape(NB, width, BS)


def reference(block_values, block_index, block_count, strength, raw_scores):
    degree = apply_graph(jnp.ones((NB, 1, BS), jnp.float32), block_values, block_index, block_count)

    def operator(field):
        return field + strength[None, :, None] * (degree * field - apply_graph(field, block_values, block_index, block_count))

    def total(field):
        return jnp.sum(field, axis=(0, 2))

    smoothed = jnp.zeros_like(raw_scores)
    residual = raw_scores
    direction = raw_scores
    norm_now = total(residual * residual)
    for iteration in range(ITERS):
        image = operator(direction)
        step_size = norm_now / total(direction * image)
        smoothed = smoothed + step_size[None, :, None] * direction
        residual = residual - step_size[None, :, None] * image
        norm_next = total(residual * residual)
        direction = residual + (norm_next / norm_now)[None, :, None] * direction
        norm_now = norm_next
    return smoothed, residual
```

```python
import functools
import jax
import jax.numpy as jnp
from jax import lax
from jax.experimental import pallas as pl
from jax.experimental.pallas import tpu as pltpu
from jax.sharding import PartitionSpec as P

BF = jnp.bfloat16
F32 = jnp.float32
VMEM = pl.BlockSpec(memory_space=pltpu.VMEM)
SMEM = pl.BlockSpec(memory_space=pltpu.SMEM)
GROUP = 8


def split_kernel(meta_ref, values_ref, out_ref):
    first = pl.program_id(0) * values_ref.shape[0]
    size = values_ref.shape[1]

    def write(turn):
        for slot in range(values_ref.shape[0]):
            block = values_ref[slot]
            block = jnp.where(first + slot < meta_ref[1], block, 0.0)
            block = block.T if turn else block
            high = block.astype(BF)
            out_ref[slot, :size] = high
            out_ref[slot, size:] = (block - high.astype(F32)).astype(BF)

    @pl.when(meta_ref[0] == 0)
    def _():
        write(True)

    @pl.when(meta_ref[0] != 0)
    def _():
        write(False)


def split_blocks(values, core, count):
    slots, size, _ = values.shape
    step = GROUP
    return pl.pallas_call(
        split_kernel,
        grid=(slots // step,),
        in_specs=[SMEM, pl.BlockSpec((step, size, size), lambda i: (i, 0, 0))],
        out_specs=pl.BlockSpec((step, 2 * size, size), lambda i: (i, 0, 0)),
        out_shape=jax.ShapeDtypeStruct((slots, 2 * size, size), BF),
        compiler_params=pltpu.CompilerParams(vmem_limit_bytes=32 * 2**20),
        cost_estimate=pl.CostEstimate(
            flops=slots * size * size * 4, bytes_accessed=slots * size * size * 8, transcendentals=0
        ),
    )(jnp.stack([core, count]), values)


def apply_kernel(parts, with_degree, with_aux, *refs):
    meta_ref, own_ref, other_ref = refs[:3]
    fields = refs[3 : 3 + parts]
    outs = refs[3 + parts : 3 + 2 * parts]
    stack_ref, sum_ref = refs[3 + 2 * parts :]
    per = outs[0].shape[0] - 1
    width, size = fields[0].shape[1:]
    for part in range(parts):
        for j in range(per):
            x = fields[part][j]
            high = x.astype(BF)
            low = (x - high.astype(F32)).astype(BF)
            f = part * per + j
            for half in range(2):
                cut = slice(half * size, (half + 1) * size)
                stack_ref[f, :width, cut] = high
                stack_ref[f, width : 2 * width, cut] = low
            if with_degree:
                stack_ref[f, 2 * width :, :] = jnp.ones((16, 2 * size), BF)
    sum_ref[...] = jnp.zeros_like(sum_ref)
    slots = own_ref.shape[0]

    def sweep(values_ref, base, count):
        def group(g, carry):
            products = []
            for i in range(GROUP):
                q = g * GROUP + i
                products.append(
                    jnp.dot(
                        stack_ref[meta_ref[0, base + q]],
                        values_ref[q],
                        preferred_element_type=F32,
                    )
                )
            for i in range(GROUP):
                to = meta_ref[1, base + g * GROUP + i]
                whole = products[i]
                sum_ref[to, :width] += whole[:width] + whole[width : 2 * width]
                if with_degree:
                    sum_ref[to, width:] += whole[2 * width : 2 * width + 8]
            return carry

        lax.fori_loop(0, (count + GROUP - 1) // GROUP, group, 0)

    sweep(own_ref, 0, meta_ref[2, 0])
    sweep(other_ref, slots, meta_ref[2, 1])
    if with_aux:
        aux = fields[0][per]
        for part in range(1, parts):
            aux = aux + fields[part][per]
    for part in range(parts):
        for j in range(per):
            outs[part][j] = sum_ref[part * per + j, :width]
        if with_aux:
            outs[part][per] = aux
        else:
            outs[part][per] = jnp.zeros((width, size), F32)
            for j in range(per):
                outs[part][per, j : j + 1, :] = sum_ref[part * per + j, width : width + 1]


def apply_blocks(meta, own, other, fields, with_degree, with_aux):
    parts = len(fields)
    width, size = fields[0].shape[1:]
    per = fields[0].shape[0] - (1 if with_aux else 0)
    rows = 2 * width + (16 if with_degree else 0)
    sums = width + (8 if with_degree else 0)
    slots = own.shape[0]
    return pl.pallas_call(
        functools.partial(apply_kernel, parts, with_degree, with_aux),
        in_specs=[SMEM] + [VMEM] * (2 + parts),
        out_specs=[VMEM] * parts,
        out_shape=[jax.ShapeDtypeStruct((per + 1, width, size), F32)] * parts,
        scratch_shapes=[
            pltpu.VMEM((parts * per, rows, 2 * size), BF),
            pltpu.VMEM((parts * per, sums, size), F32),
        ],
        compiler_params=pltpu.CompilerParams(vmem_limit_bytes=40 * 2**20),
        cost_estimate=pl.CostEstimate(
            flops=2 * slots * 4 * rows * size * size,
            bytes_accessed=4 * slots * size * size * 2,
            transcendentals=0,
        ),
    )(meta, own, other, *fields)


def dots(*pairs):
    lane = lax.broadcasted_iota(jnp.int32, pairs[0][0].shape[1:], 1)
    aux = jnp.zeros(pairs[0][0].shape[1:], F32)
    for n, (a, b) in enumerate(pairs):
        aux = jnp.where(lane == n, jnp.sum(a * b, axis=(0, 2))[:, None], aux)
    return aux


def lane_of(aux, n):
    return aux[None, :, n : n + 1]


def build(n_row, n_col):
    n_line = n_col // 2
    parts = max(n_row, n_line)

    def joint(array, offset, row_core):
        pairs = []
        for r in range(n_row):
            for z in range(n_line):
                for k in range(2):
                    to_r, to_z = (r ^ offset, z) if k == row_core else (r, z ^ offset)
                    if to_r < n_row and to_z < n_line:
                        pairs.append((r * n_col + z * 2 + k, to_r * n_col + to_z * 2 + k))
        return lax.ppermute(array, ("row", "col"), pairs)

    def swap(array):
        return lax.ppermute(array, "col", [(c, c ^ 1) for c in range(n_col)])

    def gather(field):
        return [field] + [joint(field, offset, 0) for offset in range(1, parts)]

    def collect(sent):
        return sent[0] + sum(joint(sent[offset], offset, 1) for offset in range(1, parts))

    def shards(block_values, block_index, block_count, strength, raw_scores):
        values = block_values[0, 0]
        index = block_index[0, 0]
        count = block_count[0, 0]
        row = lax.axis_index("row").astype(jnp.int32)
        col = lax.axis_index("col").astype(jnp.int32)
        line, core = col // 2, col % 2
        seg = raw_scores.shape[0]
        per = 2 * seg
        raw_other = swap(raw_scores)
        ints = jnp.concatenate([index, jnp.full((1, index.shape[1]), count, jnp.int32)], axis=0)
        ints_other = swap(ints)
        values_other = swap(values)

        def places(pair, home):
            row_place = ((pair[0] // per) ^ line) * per + pair[0] % per
            col_place = ((pair[1] // seg) ^ row) * per + home * seg + pair[1] % seg
            return jnp.where(
                core == 0, jnp.stack([col_place, row_place]), jnp.stack([row_place, col_place])
            )

        counts = jnp.zeros((1, 2 * index.shape[1]), jnp.int32)
        counts = counts.at[0, 0].set(count).at[0, 1].set(ints_other[2, 0])
        meta = jnp.concatenate(
            [jnp.concatenate([places(index, core), places(ints_other, 1 - core)], axis=1), counts],
            axis=0,
        )
        raw = jnp.where(
            core == 0,
            jnp.concatenate([raw_scores, raw_other]),
            jnp.concatenate([raw_other, raw_scores]),
        )
        gains = strength[None, :, None]
        gathered = gather(raw)
        own = split_blocks(values, core, count)
        other = split_blocks(values_other, core, ints_other[2, 0])

        mine = collect(apply_blocks(meta, own, other, gathered, True, False))
        both = mine + swap(mine)
        degree = both[per, :per, None, :]
        w0 = raw + gains * (degree * raw - both[:per])

        def with_aux(field, *pairs):
            return jnp.concatenate([field, dots(*pairs)[None]])

        mine = collect(
            apply_blocks(meta, own, other, gather(with_aux(w0, (raw, raw), (raw, w0))), False, True)
        )
        sums = mine[per]
        product = mine[:per] + swap(mine[:per])
        q0 = w0 + gains * (degree * w0 - product)
        gamma0, delta0 = lane_of(sums, 0), lane_of(sums, 1)
        step0 = gamma0 / delta0
        r1 = raw - step0 * w0
        w1 = w0 - step0 * q0
        h = r1 - step0 * w1

        pairs = (
            (r1, r1),
            (r1, w1),
            (r1, w0),
            (h, h),
            (h, w1),
            (h, w0),
            (w1, w1),
            (w1, w0),
            (w0, w0),
            (h, q0),
            (w1, q0),
            (w0, q0),
        )
        mine = collect(apply_blocks(meta, own, other, gather(with_aux(h, *pairs)), False, True))
        sums = mine[per]
        product = mine[:per] + swap(mine[:per])
        qh = h + gains * (degree * h - product)
        tail = dots((h, qh))
        tail = sum(gather(tail))
        tail = collect([tail] * parts)
        g11, r1w1, r1w0, hh, hw1, hw0, w11, w10, w00, a_h0, a_10, a_00 = (
            lane_of(sums, n) for n in range(len(pairs))
        )
        a_hh = lane_of(tail, 0)
        ratio0 = g11 / gamma0
        curve1 = r1w1 + 2.0 * ratio0 * r1w0 + ratio0 * ratio0 * delta0
        step1 = g11 / curve1
        e = step0 - step1
        f = -step1 * ratio0
        g22 = hh + 2.0 * (e * hw1 + f * hw0 + e * f * w10) + e * e * w11 + f * f * w00
        ratio1 = g22 / g11
        r2w1 = hw1 + e * w11 + f * w10
        r2w0 = hw0 + e * w10 + f * w00
        a_h1 = (hw1 - a_hh) / step0
        a_11 = (w11 - a_h1) / step0
        curve2 = a_hh + e * e * a_11 + f * f * a_00
        curve2 = curve2 + 2.0 * (e * a_h1 + f * a_h0 + e * f * a_10)
        curve2 = curve2 + 2.0 * ratio1 * (r2w1 + ratio0 * r2w0) + ratio1 * ratio1 * curve1
        step2 = g22 / curve2
        p1 = r1 + ratio0 * raw
        s1 = w1 + ratio0 * w0
        r2 = h + e * w1 + f * w0
        p2 = r2 + ratio1 * p1
        s2 = qh + e * (w1 - qh) / step0 + f * q0 + ratio1 * s1
        smoothed = step0 * raw + step1 * p1 + step2 * p2
        residual = r2 - step2 * s2

        def pick(field):
            return jnp.where(core == 0, field[:seg], field[seg:])

        return (pick(smoothed), pick(residual))

    return shards


def solution(mesh):
    placed = (
        P("row", "col", None, None, None),
        P("row", "col", None, None),
        P("row", "col"),
        P(),
        P(("row", "col"), None, None),
    )
    return jax.shard_map(
        build(mesh.shape["row"], mesh.shape["col"]),
        mesh=mesh,
        in_specs=placed,
        out_specs=(P(("row", "col"), None, None), P(("row", "col"), None, None)),
        check_vma=False,
    )
```

```python
import functools
import jax
import jax.numpy as jnp
from jax import lax
from jax.experimental import pallas as pl
from jax.experimental.pallas import tpu as pltpu
from jax.sharding import PartitionSpec as P

BF = jnp.bfloat16
F32 = jnp.float32
VMEM = pl.BlockSpec(memory_space=pltpu.VMEM)
SMEM = pl.BlockSpec(memory_space=pltpu.SMEM)
GROUP = 8


def core_here():
    return lax.rem(lax.axis_index("col").astype(jnp.int32), 2)


def places_kernel(seg, index_ref, count_ref, raw_ref, out_ref, raw_out_ref):
    raw_out_ref[...] = raw_ref[...]
    row = lax.axis_index("row").astype(jnp.int32)
    col = lax.axis_index("col").astype(jnp.int32)
    line, core = lax.div(col, 2), lax.rem(col, 2)
    per = 2 * seg
    seg_bits, per_bits = seg.bit_length() - 1, per.bit_length() - 1
    u = index_ref[0, 0, 0:1]
    v = index_ref[0, 0, 1:2]
    out_ref[0:1] = ((u >> per_bits) ^ line) * per + (u & (per - 1))
    out_ref[1:2] = ((v >> seg_bits) ^ row) * per + core * seg + (v & (seg - 1))
    out_ref[2:3] = jnp.zeros_like(u) + count_ref[0, 0]


def find_places(block_index, block_count, raw):
    return pl.pallas_call(
        functools.partial(places_kernel, raw.shape[0]),
        in_specs=[VMEM, SMEM, VMEM],
        out_specs=[VMEM, VMEM],
        out_shape=[
            pltpu.VMEM((3, block_index.shape[3]), jnp.int32),
            pltpu.VMEM(raw.shape, F32),
        ],
    )(block_index, block_count, raw)


def split_kernel(own_places, other_places, own_hbm, other_in, own_out, other_out, own_in, sems):
    slots, size, _ = own_in.shape
    core = core_here()
    copies = []
    for chunk in range(slots // GROUP):
        cut = pl.ds(chunk * GROUP, GROUP)
        copies.append(pltpu.make_async_copy(own_hbm.at[cut], own_in.at[cut], sems.at[chunk]))
    for copy in copies:
        copy.start()

    def write(turn):
        def sweep(places, source, target, chunk):
            @pl.when(chunk * GROUP < places[2, 0])
            def _():
                for i in range(GROUP):
                    slot = chunk * GROUP + i
                    block = jnp.where(slot < places[2, 0], source[slot], 0.0)
                    block = block.T if turn else block
                    high = block.astype(BF)
                    target[slot, :size] = high
                    target[slot, size:] = (block - high.astype(F32)).astype(BF)

        for chunk in range(slots // GROUP):
            sweep(other_places, other_in, other_out, chunk)
        for chunk in range(slots // GROUP):
            copies[chunk].wait()
            sweep(own_places, own_in, own_out, chunk)

    @pl.when(core == 0)
    def _():
        write(True)

    @pl.when(core != 0)
    def _():
        write(False)


def split_blocks(places, places_other, values, values_other):
    slots, size, _ = values.shape
    return pl.pallas_call(
        split_kernel,
        in_specs=[SMEM, SMEM, pl.BlockSpec(memory_space=pltpu.HBM), VMEM],
        out_specs=[VMEM, VMEM],
        out_shape=[pltpu.VMEM((slots, 2 * size, size), BF)] * 2,
        scratch_shapes=[
            pltpu.VMEM((slots, size, size), F32),
            pltpu.SemaphoreType.DMA((slots // GROUP,)),
        ],
        compiler_params=pltpu.CompilerParams(vmem_limit_bytes=32 * 2**20),
        cost_estimate=pl.CostEstimate(
            flops=slots * size * size * 8, bytes_accessed=slots * size * size * 16, transcendentals=0
        ),
    )(
        places,
        places_other,
        pltpu.with_memory_space_constraint(values, pltpu.HBM),
        pltpu.with_memory_space_constraint(values_other, pltpu.VMEM),
    )


def apply_kernel(parts, with_degree, with_aux, *refs):
    own_places, other_places, own_ref, other_ref = refs[:4]
    fields = refs[4 : 4 + parts]
    outs = refs[4 + parts : 4 + 2 * parts]
    stack_ref, sum_ref = refs[4 + 2 * parts :]
    per = outs[0].shape[0] - 1
    width, size = fields[0].shape[1:]
    for part in range(parts):
        for j in range(per):
            x = fields[part][j]
            high = x.astype(BF)
            low = (x - high.astype(F32)).astype(BF)
            f = part * per + j
            for half in range(2):
                cut = slice(half * size, (half + 1) * size)
                stack_ref[f, :width, cut] = high
                stack_ref[f, width : 2 * width, cut] = low
            if with_degree:
                stack_ref[f, 2 * width :, :] = jnp.ones((16, 2 * size), BF)
    sum_ref[...] = jnp.zeros_like(sum_ref)
    core = core_here()

    def sweep(values_ref, places):
        count = places[2, 0]

        def group(g, carry):
            products = []
            for i in range(GROUP):
                q = g * GROUP + i
                products.append(
                    jnp.dot(
                        stack_ref[places[1 - core, q]],
                        values_ref[q],
                        preferred_element_type=F32,
                    )
                )
            for i in range(GROUP):
                to = places[core, g * GROUP + i]
                whole = products[i]
                sum_ref[to, :width] += whole[:width] + whole[width : 2 * width]
                if with_degree:
                    sum_ref[to, width:] += whole[2 * width : 2 * width + 8]
            return carry

        lax.fori_loop(0, (count + GROUP - 1) // GROUP, group, 0)

    sweep(own_ref, own_places)
    sweep(other_ref, other_places)
    if with_aux:
        aux = fields[0][per]
        for part in range(1, parts):
            aux = aux + fields[part][per]
    for part in range(parts):
        for j in range(per):
            outs[part][j] = sum_ref[part * per + j, :width]
        if with_aux:
            outs[part][per] = aux
        else:
            outs[part][per] = jnp.zeros((width, size), F32)
            for j in range(per):
                outs[part][per, j : j + 1, :] = sum_ref[part * per + j, width : width + 1]


def apply_blocks(matrix, fields, with_degree, with_aux):
    parts = len(fields)
    width, size = fields[0].shape[1:]
    per = fields[0].shape[0] - (1 if with_aux else 0)
    rows = 2 * width + (16 if with_degree else 0)
    sums = width + (8 if with_degree else 0)
    slots = matrix[2].shape[0]
    return pl.pallas_call(
        functools.partial(apply_kernel, parts, with_degree, with_aux),
        in_specs=[SMEM] * 2 + [VMEM] * (2 + parts),
        out_specs=[VMEM] * parts,
        out_shape=[jax.ShapeDtypeStruct((per + 1, width, size), F32)] * parts,
        scratch_shapes=[
            pltpu.VMEM((parts * per, rows, 2 * size), BF),
            pltpu.VMEM((parts * per, sums, size), F32),
        ],
        compiler_params=pltpu.CompilerParams(vmem_limit_bytes=40 * 2**20),
        cost_estimate=pl.CostEstimate(
            flops=2 * slots * 4 * rows * size * size,
            bytes_accessed=4 * slots * size * size * 2,
            transcendentals=0,
        ),
    )(*matrix, *fields)


def dots(*pairs):
    lane = lax.broadcasted_iota(jnp.int32, pairs[0][0].shape[1:], 1)
    aux = jnp.zeros(pairs[0][0].shape[1:], F32)
    for n, (a, b) in enumerate(pairs):
        aux = jnp.where(lane == n, jnp.sum(a * b, axis=(0, 2))[:, None], aux)
    return aux


def lane_of(aux, n):
    return aux[None, :, n : n + 1]


def build(n_row, n_col):
    n_line = n_col // 2
    parts = max(n_row, n_line)

    def joint(array, offset, row_core):
        pairs = []
        for r in range(n_row):
            for z in range(n_line):
                for k in range(2):
                    to_r, to_z = (r ^ offset, z) if k == row_core else (r, z ^ offset)
                    if to_r < n_row and to_z < n_line:
                        pairs.append((r * n_col + z * 2 + k, to_r * n_col + to_z * 2 + k))
        return lax.ppermute(array, ("row", "col"), pairs)

    def swap(array):
        return lax.ppermute(array, "col", [(c, c ^ 1) for c in range(n_col)])

    def gather(field):
        return [field] + [joint(field, offset, 0) for offset in range(1, parts)]

    def collect(sent):
        return sent[0] + sum(joint(sent[offset], offset, 1) for offset in range(1, parts))

    def shards(block_values, block_index, block_count, strength, raw_scores):
        values = block_values[0, 0]
        core = core_here()
        seg = raw_scores.shape[0]
        per = 2 * seg
        raw_other = swap(raw_scores)
        places, raw_own = find_places(block_index, block_count, raw_scores)
        raw_other, raw_own, later_values = lax.optimization_barrier((raw_other, raw_own, values))
        values_other = swap(later_values)
        raw = jnp.where(
            core == 0,
            jnp.concatenate([raw_own, raw_other]),
            jnp.concatenate([raw_other, raw_own]),
        )
        places_other = swap(places)
        gains = strength[None, :, None]
        gathered = gather(raw)
        values, values_other = lax.optimization_barrier((values, values_other))
        matrix = (places, places_other) + tuple(
            split_blocks(places, places_other, values, values_other)
        )

        mine = collect(apply_blocks(matrix, gathered, True, False))
        both = mine + swap(mine)
        degree = both[per, :per, None, :]
        w0 = raw + gains * (degree * raw - both[:per])

        def with_aux(field, *pairs):
            return jnp.concatenate([field, dots(*pairs)[None]])

        mine = collect(
            apply_blocks(matrix, gather(with_aux(w0, (raw, raw), (raw, w0))), False, True)
        )
        sums = mine[per]
        product = mine[:per] + swap(mine[:per])
        q0 = w0 + gains * (degree * w0 - product)
        gamma0, delta0 = lane_of(sums, 0), lane_of(sums, 1)
        step0 = gamma0 / delta0
        r1 = raw - step0 * w0
        w1 = w0 - step0 * q0
        h = r1 - step0 * w1

        pairs = (
            (r1, r1),
            (r1, w1),
            (r1, w0),
            (h, h),
            (h, w1),
            (h, w0),
            (w1, w1),
            (w1, w0),
            (w0, w0),
            (h, q0),
            (w1, q0),
            (w0, q0),
        )
        mine = collect(apply_blocks(matrix, gather(with_aux(h, *pairs)), False, True))
        sums = mine[per]
        product = mine[:per] + swap(mine[:per])
        qh = h + gains * (degree * h - product)
        tail = dots((h, qh))
        tail = sum(gather(tail))
        tail = collect([tail] * parts)
        g11, r1w1, r1w0, hh, hw1, hw0, w11, w10, w00, a_h0, a_10, a_00 = (
            lane_of(sums, n) for n in range(len(pairs))
        )
        a_hh = lane_of(tail, 0)
        ratio0 = g11 / gamma0
        curve1 = r1w1 + 2.0 * ratio0 * r1w0 + ratio0 * ratio0 * delta0
        step1 = g11 / curve1
        e = step0 - step1
        f = -step1 * ratio0
        g22 = hh + 2.0 * (e * hw1 + f * hw0 + e * f * w10) + e * e * w11 + f * f * w00
        ratio1 = g22 / g11
        r2w1 = hw1 + e * w11 + f * w10
        r2w0 = hw0 + e * w10 + f * w00
        a_h1 = (hw1 - a_hh) / step0
        a_11 = (w11 - a_h1) / step0
        curve2 = a_hh + e * e * a_11 + f * f * a_00
        curve2 = curve2 + 2.0 * (e * a_h1 + f * a_h0 + e * f * a_10)
        curve2 = curve2 + 2.0 * ratio1 * (r2w1 + ratio0 * r2w0) + ratio1 * ratio1 * curve1
        step2 = g22 / curve2
        p1 = r1 + ratio0 * raw
        s1 = w1 + ratio0 * w0
        r2 = h + e * w1 + f * w0
        p2 = r2 + ratio1 * p1
        s2 = qh + e * (w1 - qh) / step0 + f * q0 + ratio1 * s1
        smoothed = step0 * raw + step1 * p1 + step2 * p2
        residual = r2 - step2 * s2

        def pick(field):
            return jnp.where(core == 0, field[:seg], field[seg:])

        return (pick(smoothed), pick(residual))

    return shards


def solution(mesh):
    placed = (
        P("row", "col", None, None, None),
        P("row", "col", None, None),
        P("row", "col"),
        P(),
        P(("row", "col"), None, None),
    )
    return jax.shard_map(
        build(mesh.shape["row"], mesh.shape["col"]),
        mesh=mesh,
        in_specs=placed,
        out_specs=(P(("row", "col"), None, None), P(("row", "col"), None, None)),
        check_vma=False,
    )
```

```python
import functools
import jax
import jax.numpy as jnp
from jax import lax
from jax.experimental import pallas as pl
from jax.experimental.pallas import tpu as pltpu
from jax.sharding import PartitionSpec as P

BF = jnp.bfloat16
F32 = jnp.float32
VMEM = pl.BlockSpec(memory_space=pltpu.VMEM)
SMEM = pl.BlockSpec(memory_space=pltpu.SMEM)
GROUP = 8


def core_here():
    return lax.rem(lax.axis_index("col").astype(jnp.int32), 2)


def places_kernel(seg, index_ref, count_ref, raw_ref, out_ref, raw_out_ref):
    raw_out_ref[...] = raw_ref[...]
    row = lax.axis_index("row").astype(jnp.int32)
    col = lax.axis_index("col").astype(jnp.int32)
    line, core = lax.div(col, 2), lax.rem(col, 2)
    per = 2 * seg
    seg_bits, per_bits = seg.bit_length() - 1, per.bit_length() - 1
    u = index_ref[0, 0, 0:1]
    v = index_ref[0, 0, 1:2]
    out_ref[0:1] = ((u >> per_bits) ^ line) * per + (u & (per - 1))
    out_ref[1:2] = ((v >> seg_bits) ^ row) * per + core * seg + (v & (seg - 1))
    out_ref[2:3] = jnp.zeros_like(u) + count_ref[0, 0]


def find_places(block_index, block_count, raw):
    return pl.pallas_call(
        functools.partial(places_kernel, raw.shape[0]),
        in_specs=[VMEM, SMEM, VMEM],
        out_specs=[VMEM, VMEM],
        out_shape=[
            pltpu.VMEM((3, block_index.shape[3]), jnp.int32),
            pltpu.VMEM(raw.shape, F32),
        ],
    )(block_index, block_count, raw)


def split_kernel(own_places, other_places, own_hbm, other_in, own_out, other_out, own_in, sems):
    slots, size, _ = own_in.shape
    core = core_here()
    copies = []
    for chunk in range(slots // GROUP):
        cut = pl.ds(chunk * GROUP, GROUP)
        copies.append(pltpu.make_async_copy(own_hbm.at[cut], own_in.at[cut], sems.at[chunk]))
    for copy in copies:
        copy.start()

    def write(turn):
        def sweep(places, source, target, chunk):
            @pl.when(chunk * GROUP < places[2, 0])
            def _():
                for i in range(GROUP):
                    slot = chunk * GROUP + i
                    block = jnp.where(slot < places[2, 0], source[slot], 0.0)
                    block = block.T if turn else block
                    high = block.astype(BF)
                    target[slot, :size] = high
                    target[slot, size:] = (block - high.astype(F32)).astype(BF)

        for chunk in range(slots // GROUP):
            sweep(other_places, other_in, other_out, chunk)
        for chunk in range(slots // GROUP):
            copies[chunk].wait()
            sweep(own_places, own_in, own_out, chunk)

    @pl.when(core == 0)
    def _():
        write(True)

    @pl.when(core != 0)
    def _():
        write(False)


def split_blocks(places, places_other, values, values_other):
    slots, size, _ = values.shape
    return pl.pallas_call(
        split_kernel,
        in_specs=[SMEM, SMEM, pl.BlockSpec(memory_space=pltpu.HBM), VMEM],
        out_specs=[VMEM, VMEM],
        out_shape=[pltpu.VMEM((slots, 2 * size, size), BF)] * 2,
        scratch_shapes=[
            pltpu.VMEM((slots, size, size), F32),
            pltpu.SemaphoreType.DMA((slots // GROUP,)),
        ],
        compiler_params=pltpu.CompilerParams(vmem_limit_bytes=32 * 2**20),
        cost_estimate=pl.CostEstimate(
            flops=slots * size * size * 8, bytes_accessed=slots * size * size * 16, transcendentals=0
        ),
    )(
        places,
        places_other,
        pltpu.with_memory_space_constraint(values, pltpu.HBM),
        pltpu.with_memory_space_constraint(values_other, pltpu.VMEM),
    )


def apply_kernel(parts, with_degree, with_aux, *refs):
    own_places, other_places, own_ref, other_ref = refs[:4]
    fields = refs[4 : 4 + parts]
    outs = refs[4 + parts : 4 + 2 * parts]
    stack_ref, sum_ref = refs[4 + 2 * parts :]
    per = outs[0].shape[0] - 1
    width, size = fields[0].shape[1:]
    for part in range(parts):
        for j in range(per):
            x = fields[part][j]
            high = x.astype(BF)
            low = (x - high.astype(F32)).astype(BF)
            f = part * per + j
            for half in range(2):
                cut = slice(half * size, (half + 1) * size)
                stack_ref[f, :width, cut] = high
                stack_ref[f, width : 2 * width, cut] = low
            if with_degree:
                stack_ref[f, 2 * width :, :] = jnp.ones((16, 2 * size), BF)
    sum_ref[...] = jnp.zeros_like(sum_ref)
    core = core_here()

    def sweep(values_ref, places):
        count = places[2, 0]

        def group(g, carry):
            products = []
            for i in range(GROUP):
                q = g * GROUP + i
                products.append(
                    jnp.dot(
                        stack_ref[places[1 - core, q]],
                        values_ref[q],
                        preferred_element_type=F32,
                    )
                )
            for i in range(GROUP):
                to = places[core, g * GROUP + i]
                whole = products[i]
                sum_ref[to, :width] += whole[:width] + whole[width : 2 * width]
                if with_degree:
                    sum_ref[to, width:] += whole[2 * width : 2 * width + 8]
            return carry

        lax.fori_loop(0, (count + GROUP - 1) // GROUP, group, 0)

    sweep(own_ref, own_places)
    sweep(other_ref, other_places)
    if with_aux:
        aux = fields[0][per]
        for part in range(1, parts):
            aux = aux + fields[part][per]
    for part in range(parts):
        for j in range(per):
            outs[part][j] = sum_ref[part * per + j, :width]
        if with_aux:
            outs[part][per] = aux
        else:
            outs[part][per] = jnp.zeros((width, size), F32)
            for j in range(per):
                outs[part][per, j : j + 1, :] = sum_ref[part * per + j, width : width + 1]


def apply_blocks(matrix, fields, with_degree, with_aux):
    parts = len(fields)
    width, size = fields[0].shape[1:]
    per = fields[0].shape[0] - (1 if with_aux else 0)
    rows = 2 * width + (16 if with_degree else 0)
    sums = width + (8 if with_degree else 0)
    slots = matrix[2].shape[0]
    return pl.pallas_call(
        functools.partial(apply_kernel, parts, with_degree, with_aux),
        in_specs=[SMEM] * 2 + [VMEM] * (2 + parts),
        out_specs=[VMEM] * parts,
        out_shape=[jax.ShapeDtypeStruct((per + 1, width, size), F32)] * parts,
        scratch_shapes=[
            pltpu.VMEM((parts * per, rows, 2 * size), BF),
            pltpu.VMEM((parts * per, sums, size), F32),
        ],
        compiler_params=pltpu.CompilerParams(vmem_limit_bytes=40 * 2**20),
        cost_estimate=pl.CostEstimate(
            flops=2 * slots * 4 * rows * size * size,
            bytes_accessed=4 * slots * size * size * 2,
            transcendentals=0,
        ),
    )(*matrix, *fields)


def dots(*pairs):
    lane = lax.broadcasted_iota(jnp.int32, pairs[0][0].shape[1:], 1)
    aux = jnp.zeros(pairs[0][0].shape[1:], F32)
    for n, (a, b) in enumerate(pairs):
        aux = jnp.where(lane == n, jnp.sum(a * b, axis=(0, 2))[:, None], aux)
    return aux


def lane_of(aux, n):
    return aux[None, :, n : n + 1]


def build(n_row, n_col):
    n_line = n_col // 2
    parts = max(n_row, n_line)

    def joint(array, offset, row_core):
        pairs = []
        for r in range(n_row):
            for z in range(n_line):
                for k in range(2):
                    to_r, to_z = (r ^ offset, z) if k == row_core else (r, z ^ offset)
                    if to_r < n_row and to_z < n_line:
                        pairs.append((r * n_col + z * 2 + k, to_r * n_col + to_z * 2 + k))
        return lax.ppermute(array, ("row", "col"), pairs)

    def swap(array):
        return lax.ppermute(array, "col", [(c, c ^ 1) for c in range(n_col)])

    def gather(field):
        return [field] + [joint(field, offset, 0) for offset in range(1, parts)]

    def collect(sent):
        return sent[0] + sum(joint(sent[offset], offset, 1) for offset in range(1, parts))

    def shards(block_values, block_index, block_count, strength, raw_scores):
        values = block_values[0, 0]
        core = core_here()
        seg = raw_scores.shape[0]
        per = 2 * seg
        raw_other = swap(raw_scores)
        places, raw_own = find_places(block_index, block_count, raw_scores)
        raw_other, raw_own, later_values = lax.optimization_barrier((raw_other, raw_own, values))
        values_other = swap(later_values)
        raw = jnp.where(
            core == 0,
            jnp.concatenate([raw_own, raw_other]),
            jnp.concatenate([raw_other, raw_own]),
        )
        places_other = swap(places)
        gains = strength[None, :, None]
        gathered = gather(raw)
        values, values_other = lax.optimization_barrier((values, values_other))
        matrix = (places, places_other) + tuple(
            split_blocks(places, places_other, values, values_other)
        )

        mine = collect(apply_blocks(matrix, gathered, True, False))
        both = mine + swap(mine)
        degree = both[per, :per, None, :]
        w0 = raw + gains * (degree * raw - both[:per])

        def with_aux(field, *pairs):
            return jnp.concatenate([field, dots(*pairs)[None]])

        mine = collect(
            apply_blocks(matrix, gather(with_aux(w0, (raw, raw), (raw, w0))), False, True)
        )
        sums = mine[per]
        product = mine[:per] + swap(mine[:per])
        q0 = w0 + gains * (degree * w0 - product)
        gamma0, delta0 = lane_of(sums, 0), lane_of(sums, 1)
        step0 = gamma0 / delta0
        r1 = raw - step0 * w0
        w1 = w0 - step0 * q0
        h = r1 - step0 * w1

        pairs = (
            (r1, r1),
            (r1, w1),
            (r1, w0),
            (h, h),
            (h, w1),
            (h, w0),
            (w1, w1),
            (w1, w0),
            (w0, w0),
            (h, q0),
            (w1, q0),
            (w0, q0),
            (degree * h, h),
        )
        gathered = gather(with_aux(h, *pairs))
        crossed = swap(jnp.concatenate(gathered[1:]))
        crossed = [gathered[0]] + jnp.split(crossed, parts - 1)
        sent = apply_blocks(matrix, gathered, False, True)
        cross = sum(
            jnp.sum(out[:per] * part[:per], axis=(0, 2)) for out, part in zip(sent, crossed)
        )
        lane = lax.broadcasted_iota(jnp.int32, h.shape[1:], 1)
        cross = jnp.where(lane == len(pairs), cross[:, None], 0.0)
        sent = [jnp.concatenate([out[:per], (out[per] + cross)[None]]) for out in sent]
        mine = collect(sent)
        sums = mine[per]
        tail = sum(gather(sums))
        product = mine[:per] + swap(mine[:per])
        qh = h + gains * (degree * h - product)
        g11, r1w1, r1w0, hh, hw1, hw0, w11, w10, w00, a_h0, a_10, a_00, hdh = (
            lane_of(sums, n) for n in range(len(pairs))
        )
        a_hh = hh + gains * (hdh - 2.0 * lane_of(tail, len(pairs)))
        ratio0 = g11 / gamma0
        curve1 = r1w1 + 2.0 * ratio0 * r1w0 + ratio0 * ratio0 * delta0
        step1 = g11 / curve1
        e = step0 - step1
        f = -step1 * ratio0
        g22 = hh + 2.0 * (e * hw1 + f * hw0 + e * f * w10) + e * e * w11 + f * f * w00
        ratio1 = g22 / g11
        r2w1 = hw1 + e * w11 + f * w10
        r2w0 = hw0 + e * w10 + f * w00
        a_h1 = (hw1 - a_hh) / step0
        a_11 = (w11 - a_h1) / step0
        curve2 = a_hh + e * e * a_11 + f * f * a_00
        curve2 = curve2 + 2.0 * (e * a_h1 + f * a_h0 + e * f * a_10)
        curve2 = curve2 + 2.0 * ratio1 * (r2w1 + ratio0 * r2w0) + ratio1 * ratio1 * curve1
        step2 = g22 / curve2
        p1 = r1 + ratio0 * raw
        s1 = w1 + ratio0 * w0
        r2 = h + e * w1 + f * w0
        p2 = r2 + ratio1 * p1
        s2 = qh + e * (w1 - qh) / step0 + f * q0 + ratio1 * s1
        smoothed = step0 * raw + step1 * p1 + step2 * p2
        residual = r2 - step2 * s2

        def pick(field):
            return jnp.where(core == 0, field[:seg], field[seg:])

        return (pick(smoothed), pick(residual))

    return shards


def solution(mesh):
    placed = (
        P("row", "col", None, None, None),
        P("row", "col", None, None),
        P("row", "col"),
        P(),
        P(("row", "col"), None, None),
    )
    return jax.shard_map(
        build(mesh.shape["row"], mesh.shape["col"]),
        mesh=mesh,
        in_specs=placed,
        out_specs=(P(("row", "col"), None, None), P(("row", "col"), None, None)),
        check_vma=False,
    )
```

```python
import functools
import jax
import jax.numpy as jnp
from jax import lax
from jax.experimental import pallas as pl
from jax.experimental.pallas import tpu as pltpu
from jax.sharding import PartitionSpec as P

BF = jnp.bfloat16
F32 = jnp.float32
VMEM = pl.BlockSpec(memory_space=pltpu.VMEM)
SMEM = pl.BlockSpec(memory_space=pltpu.SMEM)
COPY = 8


def far_first(parts):
    return list(range(2, parts)) + [1]


def core_here():
    return lax.rem(lax.axis_index("col").astype(jnp.int32), 2)


def places_kernel(seg, index_ref, count_ref, raw_ref, out_ref, raw_out_ref):
    raw_out_ref[...] = raw_ref[...]
    row = lax.axis_index("row").astype(jnp.int32)
    col = lax.axis_index("col").astype(jnp.int32)
    line, core = lax.div(col, 2), lax.rem(col, 2)
    per = 2 * seg
    seg_bits, per_bits = seg.bit_length() - 1, per.bit_length() - 1
    u = index_ref[0, 0, 0:1]
    v = index_ref[0, 0, 1:2]
    out_ref[0:1] = ((u >> per_bits) ^ line) * per + (u & (per - 1))
    out_ref[1:2] = ((v >> seg_bits) ^ row) * per + core * seg + (v & (seg - 1))
    out_ref[2:3] = jnp.zeros_like(u) + count_ref[0, 0]


def find_places(block_index, block_count, raw):
    return pl.pallas_call(
        functools.partial(places_kernel, raw.shape[0]),
        in_specs=[VMEM, SMEM, VMEM],
        out_specs=[VMEM, VMEM],
        out_shape=[
            pltpu.VMEM((3, block_index.shape[3]), jnp.int32),
            pltpu.VMEM(raw.shape, F32),
        ],
    )(block_index, block_count, raw)


def split_kernel(own_places, other_places, own_hbm, other_in, own_out, other_out, own_in, sems):
    slots, size, _ = own_in.shape
    core = core_here()
    copies = []
    for chunk in range(slots // COPY):
        cut = pl.ds(chunk * COPY, COPY)
        copies.append(pltpu.make_async_copy(own_hbm.at[cut], own_in.at[cut], sems.at[chunk]))
    for copy in copies:
        copy.start()

    def write(turn):
        def sweep(places, source, target, chunk):
            live = chunk * COPY < places[2, 0]

            @pl.when(live)
            def _():
                for i in range(COPY):
                    slot = chunk * COPY + i
                    block = jnp.where(slot < places[2, 0], source[slot], 0.0)
                    block = block.T if turn else block
                    high = block.astype(BF)
                    target[slot, :size] = high
                    target[slot, size:] = (block - high.astype(F32)).astype(BF)

            @pl.when(jnp.logical_not(live))
            def _():
                target[pl.ds(chunk * COPY, COPY)] = jnp.zeros((COPY, 2 * size, size), BF)

        for chunk in range(slots // COPY):
            sweep(other_places, other_in, other_out, chunk)
        for chunk in range(slots // COPY):
            copies[chunk].wait()
            sweep(own_places, own_in, own_out, chunk)

    @pl.when(core == 0)
    def _():
        write(True)

    @pl.when(core != 0)
    def _():
        write(False)


def split_blocks(places, places_other, values, values_other):
    slots, size, _ = values.shape
    return pl.pallas_call(
        split_kernel,
        in_specs=[SMEM, SMEM, pl.BlockSpec(memory_space=pltpu.HBM), VMEM],
        out_specs=[VMEM, VMEM],
        out_shape=[pltpu.VMEM((slots, 2 * size, size), BF)] * 2,
        scratch_shapes=[
            pltpu.VMEM((slots, size, size), F32),
            pltpu.SemaphoreType.DMA((slots // COPY,)),
        ],
        compiler_params=pltpu.CompilerParams(vmem_limit_bytes=32 * 2**20),
        cost_estimate=pl.CostEstimate(
            flops=slots * size * size * 8, bytes_accessed=slots * size * size * 16, transcendentals=0
        ),
    )(
        places,
        places_other,
        pltpu.with_memory_space_constraint(values, pltpu.HBM),
        pltpu.with_memory_space_constraint(values_other, pltpu.VMEM),
    )


def apply_kernel(parts, with_degree, with_aux, *refs):
    own_places, other_places, own_ref, other_ref = refs[:4]
    fields = [refs[4]] + [None] * (parts - 1)
    for part, ref in zip(far_first(parts), refs[5:]):
        fields[part] = ref
    outs = refs[4 + parts : 4 + 2 * parts]
    stack_ref, sum_ref = refs[4 + 2 * parts :]
    per = outs[0].shape[0] - 1
    width, size = fields[0].shape[1:]
    for part in range(parts):
        for j in range(per):
            x = fields[part][j]
            high = x.astype(BF)
            low = (x - high.astype(F32)).astype(BF)
            f = part * per + j
            for half in range(2):
                cut = slice(half * size, (half + 1) * size)
                stack_ref[f, :width, cut] = high
                stack_ref[f, width : 2 * width, cut] = low
            if with_degree:
                stack_ref[f, 2 * width :, :] = jnp.ones((16, 2 * size), BF)
    sum_ref[...] = jnp.zeros_like(sum_ref)
    core = core_here()
    run = own_ref.shape[0]

    def sweep(values_ref, places):
        count = places[2, 0]

        def group(g, carry):
            products = []
            for i in range(run):
                q = g * run + i
                products.append(
                    jnp.dot(
                        stack_ref[places[1 - core, q]],
                        values_ref[q],
                        preferred_element_type=F32,
                    )
                )
            for i in range(run):
                to = places[core, g * run + i]
                whole = products[i]
                sum_ref[to, :width] += whole[:width] + whole[width : 2 * width]
                if with_degree:
                    sum_ref[to, width:] += whole[2 * width : 2 * width + 8]
            return carry

        lax.fori_loop(0, (count + run - 1) // run, group, 0)

    sweep(own_ref, own_places)
    sweep(other_ref, other_places)
    if with_aux:
        aux = fields[0][per]
        for part in range(1, parts):
            aux = aux + fields[part][per]
    for part in range(parts):
        for j in range(per):
            outs[part][j] = sum_ref[part * per + j, :width]
        if with_aux:
            outs[part][per] = aux
        else:
            outs[part][per] = jnp.zeros((width, size), F32)
            for j in range(per):
                outs[part][per, j : j + 1, :] = sum_ref[part * per + j, width : width + 1]


def apply_blocks(matrix, fields, with_degree, with_aux):
    parts = len(fields)
    width, size = fields[0].shape[1:]
    per = fields[0].shape[0] - (1 if with_aux else 0)
    rows = 2 * width + (16 if with_degree else 0)
    sums = width + (8 if with_degree else 0)
    slots = matrix[2].shape[0]
    return pl.pallas_call(
        functools.partial(apply_kernel, parts, with_degree, with_aux),
        in_specs=[SMEM] * 2 + [VMEM] * (2 + parts),
        out_specs=[VMEM] * parts,
        out_shape=[jax.ShapeDtypeStruct((per + 1, width, size), F32)] * parts,
        scratch_shapes=[
            pltpu.VMEM((parts * per, rows, 2 * size), BF),
            pltpu.VMEM((parts * per, sums, size), F32),
        ],
        compiler_params=pltpu.CompilerParams(vmem_limit_bytes=40 * 2**20),
        cost_estimate=pl.CostEstimate(
            flops=2 * slots * 4 * rows * size * size,
            bytes_accessed=4 * slots * size * size * 2,
            transcendentals=0,
        ),
    )(*matrix, fields[0], *(fields[part] for part in far_first(parts)))


def dots(*pairs):
    lane = lax.broadcasted_iota(jnp.int32, pairs[0][0].shape[1:], 1)
    aux = jnp.zeros(pairs[0][0].shape[1:], F32)
    for n, (a, b) in enumerate(pairs):
        aux = jnp.where(lane == n, jnp.sum(a * b, axis=(0, 2))[:, None], aux)
    return aux


def lane_of(aux, n):
    return aux[None, :, n : n + 1]


def build(n_row, n_col):
    n_line = n_col // 2
    parts = max(n_row, n_line)

    def joint(array, offset, row_core):
        pairs = []
        for r in range(n_row):
            for z in range(n_line):
                for k in range(2):
                    to_r, to_z = (r ^ offset, z) if k == row_core else (r, z ^ offset)
                    if to_r < n_row and to_z < n_line:
                        pairs.append((r * n_col + z * 2 + k, to_r * n_col + to_z * 2 + k))
        return lax.ppermute(array, ("row", "col"), pairs)

    def swap(array):
        return lax.ppermute(array, "col", [(c, c ^ 1) for c in range(n_col)])

    def gather(field):
        return [field] + [joint(field, offset, 0) for offset in range(1, parts)]

    def collect(sent):
        total = sent[0]
        for offset in reversed(far_first(parts)):
            total = total + joint(sent[offset], offset, 1)
        return total

    def shards(block_values, block_index, block_count, strength, raw_scores):
        values = block_values[0, 0]
        core = core_here()
        seg = raw_scores.shape[0]
        per = 2 * seg
        raw_other = swap(raw_scores)
        places, raw_own = find_places(block_index, block_count, raw_scores)
        raw_other, raw_own, later_values = lax.optimization_barrier((raw_other, raw_own, values))
        values_other = swap(later_values)
        raw = jnp.where(
            core == 0,
            jnp.concatenate([raw_own, raw_other]),
            jnp.concatenate([raw_other, raw_own]),
        )
        places_other = swap(places)
        gains = strength[None, :, None]
        gathered = gather(raw)
        values, values_other = lax.optimization_barrier((values, values_other))
        matrix = (places, places_other) + tuple(
            split_blocks(places, places_other, values, values_other)
        )

        mine = collect(apply_blocks(matrix, gathered, True, False))
        both = mine + swap(mine)
        degree = both[per, :per, None, :]
        w0 = raw + gains * (degree * raw - both[:per])

        def with_aux(field, *pairs):
            return jnp.concatenate([field, dots(*pairs)[None]])

        mine = collect(
            apply_blocks(matrix, gather(with_aux(w0, (raw, raw), (raw, w0))), False, True)
        )
        sums = mine[per]
        product = mine[:per] + swap(mine[:per])
        q0 = w0 + gains * (degree * w0 - product)
        gamma0, delta0 = lane_of(sums, 0), lane_of(sums, 1)
        step0 = gamma0 / delta0
        r1 = raw - step0 * w0
        w1 = w0 - step0 * q0
        h = r1 - step0 * w1

        pairs = (
            (r1, r1),
            (r1, w1),
            (r1, w0),
            (h, h),
            (h, w1),
            (h, w0),
            (w1, w1),
            (w1, w0),
            (w0, w0),
            (h, q0),
            (w1, q0),
            (w0, q0),
            (degree * h, h),
        )
        gathered = gather(with_aux(h, *pairs))
        crossed = swap(jnp.concatenate(gathered[1:]))
        crossed = [gathered[0]] + jnp.split(crossed, parts - 1)
        sent = apply_blocks(matrix, gathered, False, True)
        cross = sum(
            jnp.sum(out[:per] * part[:per], axis=(0, 2)) for out, part in zip(sent, crossed)
        )
        lane = lax.broadcasted_iota(jnp.int32, h.shape[1:], 1)
        cross = jnp.where(lane == len(pairs), cross[:, None], 0.0)
        sent = [jnp.concatenate([out[:per], (out[per] + cross)[None]]) for out in sent]
        mine = collect(sent)
        sums = mine[per]
        tail = sum(gather(sums))
        product = mine[:per] + swap(mine[:per])
        qh = h + gains * (degree * h - product)
        g11, r1w1, r1w0, hh, hw1, hw0, w11, w10, w00, a_h0, a_10, a_00, hdh = (
            lane_of(sums, n) for n in range(len(pairs))
        )
        a_hh = hh + gains * (hdh - 2.0 * lane_of(tail, len(pairs)))
        ratio0 = g11 / gamma0
        curve1 = r1w1 + 2.0 * ratio0 * r1w0 + ratio0 * ratio0 * delta0
        step1 = g11 / curve1
        e = step0 - step1
        f = -step1 * ratio0
        g22 = hh + 2.0 * (e * hw1 + f * hw0 + e * f * w10) + e * e * w11 + f * f * w00
        ratio1 = g22 / g11
        r2w1 = hw1 + e * w11 + f * w10
        r2w0 = hw0 + e * w10 + f * w00
        a_h1 = (hw1 - a_hh) / step0
        a_11 = (w11 - a_h1) / step0
        curve2 = a_hh + e * e * a_11 + f * f * a_00
        curve2 = curve2 + 2.0 * (e * a_h1 + f * a_h0 + e * f * a_10)
        curve2 = curve2 + 2.0 * ratio1 * (r2w1 + ratio0 * r2w0) + ratio1 * ratio1 * curve1
        step2 = g22 / curve2
        p1 = r1 + ratio0 * raw
        s1 = w1 + ratio0 * w0
        r2 = h + e * w1 + f * w0
        p2 = r2 + ratio1 * p1
        s2 = qh + e * (w1 - qh) / step0 + f * q0 + ratio1 * s1
        smoothed = step0 * raw + step1 * p1 + step2 * p2
        residual = r2 - step2 * s2

        def pick(field):
            return jnp.where(core == 0, field[:seg], field[seg:])

        return (pick(smoothed), pick(residual))

    return shards


def solution(mesh):
    placed = (
        P("row", "col", None, None, None),
        P("row", "col", None, None),
        P("row", "col"),
        P(),
        P(("row", "col"), None, None),
    )
    return jax.shard_map(
        build(mesh.shape["row"], mesh.shape["col"]),
        mesh=mesh,
        in_specs=placed,
        out_specs=(P(("row", "col"), None, None), P(("row", "col"), None, None)),
        check_vma=False,
    )
```

```python
import functools
import jax
import jax.numpy as jnp
from jax import lax
from jax.experimental import pallas as pl
from jax.experimental.pallas import tpu as pltpu
from jax.sharding import PartitionSpec as P

BF = jnp.bfloat16
F32 = jnp.float32
VMEM = pl.BlockSpec(memory_space=pltpu.VMEM)
SMEM = pl.BlockSpec(memory_space=pltpu.SMEM)
COPY = 8


def far_first(parts):
    return list(range(2, parts)) + [1]


def core_here():
    return lax.rem(lax.axis_index("col").astype(jnp.int32), 2)


def places_kernel(seg, index_ref, count_ref, raw_ref, out_ref, raw_out_ref):
    raw_out_ref[...] = raw_ref[...]
    row = lax.axis_index("row").astype(jnp.int32)
    col = lax.axis_index("col").astype(jnp.int32)
    line, core = lax.div(col, 2), lax.rem(col, 2)
    per = 2 * seg
    seg_bits, per_bits = seg.bit_length() - 1, per.bit_length() - 1
    u = index_ref[0, 0, 0:1]
    v = index_ref[0, 0, 1:2]
    out_ref[0:1] = ((u >> per_bits) ^ line) * per + (u & (per - 1))
    out_ref[1:2] = ((v >> seg_bits) ^ row) * per + core * seg + (v & (seg - 1))
    out_ref[2:3] = jnp.broadcast_to(count_ref[...], u.shape)


def find_places(block_index, block_count, raw):
    return pl.pallas_call(
        functools.partial(places_kernel, raw.shape[0]),
        in_specs=[VMEM, VMEM, VMEM],
        out_specs=[VMEM, VMEM],
        out_shape=[
            pltpu.VMEM((3, block_index.shape[3]), jnp.int32),
            pltpu.VMEM(raw.shape, F32),
        ],
    )(block_index, block_count, raw)


def split_kernel(own_places, other_places, own_hbm, other_in, own_out, other_out, own_in, sems):
    slots, size, _ = own_in.shape
    core = core_here()
    copies = []
    for chunk in range(slots // COPY):
        cut = pl.ds(chunk * COPY, COPY)
        copies.append(pltpu.make_async_copy(own_hbm.at[cut], own_in.at[cut], sems.at[chunk]))
    for copy in copies:
        copy.start()

    def write(turn):
        def sweep(places, source, target, chunk):
            live = chunk * COPY < places[2, 0]

            @pl.when(live)
            def _():
                for i in range(COPY):
                    slot = chunk * COPY + i
                    block = jnp.where(slot < places[2, 0], source[slot], 0.0)
                    block = block.T if turn else block
                    high = block.astype(BF)
                    target[slot, :size] = high
                    target[slot, size:] = (block - high.astype(F32)).astype(BF)

            @pl.when(jnp.logical_not(live))
            def _():
                target[pl.ds(chunk * COPY, COPY)] = jnp.zeros((COPY, 2 * size, size), BF)

        for chunk in range(slots // COPY):
            sweep(other_places, other_in, other_out, chunk)
        for chunk in range(slots // COPY):
            copies[chunk].wait()
            sweep(own_places, own_in, own_out, chunk)

    @pl.when(core == 0)
    def _():
        write(True)

    @pl.when(core != 0)
    def _():
        write(False)


def split_blocks(places, places_other, values, values_other):
    slots, size, _ = values.shape
    return pl.pallas_call(
        split_kernel,
        in_specs=[SMEM, SMEM, pl.BlockSpec(memory_space=pltpu.HBM), VMEM],
        out_specs=[VMEM, VMEM],
        out_shape=[pltpu.VMEM((slots, 2 * size, size), BF)] * 2,
        scratch_shapes=[
            pltpu.VMEM((slots, size, size), F32),
            pltpu.SemaphoreType.DMA((slots // COPY,)),
        ],
        compiler_params=pltpu.CompilerParams(vmem_limit_bytes=16 * 2**20),
        cost_estimate=pl.CostEstimate(
            flops=slots * size * size * 8, bytes_accessed=slots * size * size * 16, transcendentals=0
        ),
    )(
        places,
        places_other,
        pltpu.with_memory_space_constraint(values, pltpu.HBM),
        pltpu.with_memory_space_constraint(values_other, pltpu.VMEM),
    )


def apply_kernel(parts, per, width, with_degree, *refs):
    own_places, other_places, own_ref, other_ref = refs[:4]
    fields = [refs[4]] + [None] * (parts - 1)
    for part, ref in zip(far_first(parts), refs[5:]):
        fields[part] = ref
    outs = refs[4 + parts : 4 + 2 * parts]
    stack_ref, sum_ref = refs[4 + 2 * parts :]
    size = fields[0].shape[1]
    deep = per * width
    for part in range(parts):
        for j in range(per):
            x = fields[part][j * width : (j + 1) * width]
            high = x.astype(BF)
            low = (x - high.astype(F32)).astype(BF)
            f = part * per + j
            for half in range(2):
                cut = slice(half * size, (half + 1) * size)
                stack_ref[f, :width, cut] = high
                stack_ref[f, width : 2 * width, cut] = low
            if with_degree:
                stack_ref[f, 2 * width :, :] = jnp.ones((16, 2 * size), BF)
    sum_ref[...] = jnp.zeros_like(sum_ref)
    core = core_here()
    run = own_ref.shape[0]

    def sweep(values_ref, places):
        @pl.when(places[2, 0] > 0)
        def _():
            products = []
            for q in range(run):
                products.append(
                    jnp.dot(
                        stack_ref[places[1 - core, q]],
                        values_ref[q],
                        preferred_element_type=F32,
                    )
                )
            for q in range(run):
                to = places[core, q]
                whole = products[q]
                sum_ref[to, :width] += whole[:width] + whole[width : 2 * width]
                if with_degree:
                    sum_ref[to, width:] += whole[2 * width : 2 * width + 8]

    sweep(own_ref, own_places)
    sweep(other_ref, other_places)
    if not with_degree:
        aux = fields[0][deep:]
        for part in range(1, parts):
            aux = aux + fields[part][deep:]
    for part in range(parts):
        for j in range(per):
            outs[part][j * width : (j + 1) * width] = sum_ref[part * per + j, :width]
        if with_degree:
            outs[part][deep:] = jnp.zeros((8, size), F32)
            for j in range(per):
                row = deep + j
                outs[part][row : row + 1] = sum_ref[part * per + j, width : width + 1]
        else:
            outs[part][deep:] = aux


def apply_blocks(matrix, fields, per, width, with_degree):
    parts = len(fields)
    size = fields[0].shape[1]
    extra = 8 if with_degree else fields[0].shape[0] - per * width
    rows = 2 * width + (16 if with_degree else 0)
    sums = width + (8 if with_degree else 0)
    slots = matrix[2].shape[0]
    return pl.pallas_call(
        functools.partial(apply_kernel, parts, per, width, with_degree),
        in_specs=[SMEM] * 2 + [VMEM] * (2 + parts),
        out_specs=[VMEM] * parts,
        out_shape=[jax.ShapeDtypeStruct((per * width + extra, size), F32)] * parts,
        scratch_shapes=[
            pltpu.VMEM((parts * per, rows, 2 * size), BF),
            pltpu.VMEM((parts * per, sums, size), F32),
        ],
        compiler_params=pltpu.CompilerParams(vmem_limit_bytes=16 * 2**20),
        cost_estimate=pl.CostEstimate(
            flops=2 * slots * 4 * rows * size * size,
            bytes_accessed=4 * slots * size * size * 2,
            transcendentals=0,
        ),
    )(*matrix, fields[0], *(fields[part] for part in far_first(parts)))


def dot_rows(pairs, depth):
    width, size = pairs[0][0][0].shape
    lane = lax.broadcasted_iota(jnp.int32, (width, size), 1)
    table = jnp.zeros((width, size), F32)
    for n, (a, b) in enumerate(pairs):
        product = a[0] * b[0]
        for x, y in zip(a[1:], b[1:]):
            product = product + x * y
        table = jnp.where(lane == n, jnp.sum(product, axis=1, keepdims=True), table)
    square = jnp.concatenate([table, jnp.zeros((size - width, size), F32)], axis=0)
    return square.T[:depth]


def blocks_in(ref, per, width):
    return [ref[j * width : (j + 1) * width] for j in range(per)]


def put(ref, blocks):
    width = blocks[0].shape[0]
    for j, block in enumerate(blocks):
        ref[j * width : (j + 1) * width] = block


def first_update(per, mine, other, raw_ref, gain_ref, w0_out, degree_out, sent_out):
    width = raw_ref.shape[0] // per
    deep = per * width
    raw = blocks_in(raw_ref, per, width)
    degree = mine[deep:] + other[deep:]
    degree_out[...] = degree
    gain = gain_ref[...]
    w0 = []
    for j in range(per):
        cut = slice(j * width, (j + 1) * width)
        product = mine[cut] + other[cut]
        w0.append(raw[j] + gain * (degree[j : j + 1] * raw[j] - product))
    put(w0_out, w0)
    put(sent_out, w0)
    sent_out[deep:] = dot_rows([(raw, raw), (raw, w0)], sent_out.shape[0] - deep)


def second_update(per, mine, other, raw_ref, w0_ref, degree_ref, gain_ref, q0_out, r1_out, w1_out, sent_out):
    width = raw_ref.shape[0] // per
    deep = per * width
    raw, w0 = blocks_in(raw_ref, per, width), blocks_in(w0_ref, per, width)
    totals = jnp.concatenate(
        [mine[deep:], jnp.zeros((mine.shape[1] - mine.shape[0] + deep, mine.shape[1]), F32)]
    ).T[:width]
    step0 = totals[:, 0:1] / totals[:, 1:2]
    degree, gain = degree_ref[...], gain_ref[...]
    q0, r1, w1, h, dh = [], [], [], [], []
    for j in range(per):
        cut = slice(j * width, (j + 1) * width)
        product = mine[cut] + other[cut]
        q0.append(w0[j] + gain * (degree[j : j + 1] * w0[j] - product))
        r1.append(raw[j] - step0 * w0[j])
        w1.append(w0[j] - step0 * q0[j])
        h.append(r1[j] - step0 * w1[j])
        dh.append(degree[j : j + 1] * h[j])
    put(q0_out, q0)
    put(r1_out, r1)
    put(w1_out, w1)
    put(sent_out, h)
    pairs = (
        (r1, r1),
        (r1, w1),
        (r1, w0),
        (h, h),
        (h, w1),
        (h, w0),
        (w1, w1),
        (w1, w0),
        (w0, w0),
        (h, q0),
        (w1, q0),
        (w0, q0),
        (dh, h),
    )
    sent_out[deep:] = dot_rows(pairs, sent_out.shape[0] - deep)


def update(kernel, per, shapes, *arrays):
    return pl.pallas_call(
        functools.partial(kernel, per),
        in_specs=[VMEM] * len(arrays),
        out_specs=[VMEM] * len(shapes),
        out_shape=[pltpu.VMEM(shape, F32) for shape in shapes],
        compiler_params=pltpu.CompilerParams(vmem_limit_bytes=16 * 2**20),
    )(*arrays)


def build(n_row, n_col):
    n_line = n_col // 2
    parts = max(n_row, n_line)

    def joint(array, offset, row_core):
        pairs = []
        for r in range(n_row):
            for z in range(n_line):
                for k in range(2):
                    to_r, to_z = (r ^ offset, z) if k == row_core else (r, z ^ offset)
                    if to_r < n_row and to_z < n_line:
                        pairs.append((r * n_col + z * 2 + k, to_r * n_col + to_z * 2 + k))
        return lax.ppermute(array, ("row", "col"), pairs)

    def swap(array):
        return lax.ppermute(array, "col", [(c, c ^ 1) for c in range(n_col)])

    def gather(field):
        return [field] + [joint(field, offset, 0) for offset in range(1, parts)]

    def collect(sent):
        total = sent[0]
        for offset in reversed(far_first(parts)):
            total = total + joint(sent[offset], offset, 1)
        return total

    def shards(block_values, block_index, block_count, strength, raw_scores):
        values = block_values[0, 0]
        core = core_here()
        seg = raw_scores.shape[0]
        per = 2 * seg
        raw_other = swap(raw_scores)
        places, raw_own = find_places(block_index, block_count, raw_scores)
        raw_other, raw_own, later_values = lax.optimization_barrier((raw_other, raw_own, values))
        values_other = swap(later_values)
        raw = jnp.where(
            core == 0,
            jnp.concatenate([raw_own, raw_other]),
            jnp.concatenate([raw_other, raw_own]),
        )
        places_other = swap(places)
        gains = strength[None, :, None]
        gathered = gather(raw.reshape(per * raw.shape[1], raw.shape[2]))
        values, values_other = lax.optimization_barrier((values, values_other))
        matrix = (places, places_other) + tuple(
            split_blocks(places, places_other, values, values_other)
        )

        width, size = raw.shape[1:]
        deep = per * width

        def blocks(array):
            return array[:deep].reshape(per, width, size)

        def row_of(aux, n):
            return aux[n, :width][None, :, None]

        flat = raw.reshape(deep, size)
        gain_rows = jnp.broadcast_to(strength[:, None], (width, size))
        deep_shape, aux_rows = (deep, size), 16

        mine = collect(apply_blocks(matrix, gathered, per, width, True))
        w0, degree, sent = update(
            first_update,
            per,
            (deep_shape, (8, size), (deep + aux_rows, size)),
            mine,
            swap(mine),
            flat,
            gain_rows,
        )

        mine = collect(apply_blocks(matrix, gather(sent), per, width, False))
        gamma0, delta0 = row_of(mine[deep:], 0), row_of(mine[deep:], 1)
        step0 = gamma0 / delta0
        q0, r1, w1, sent = update(
            second_update,
            per,
            (deep_shape,) * 3 + ((deep + aux_rows, size),),
            mine,
            swap(mine[:deep]),
            flat,
            w0,
            degree,
            gain_rows,
        )
        h = blocks(sent)
        w0, q0, r1, w1 = blocks(w0), blocks(q0), blocks(r1), blocks(w1)
        degree = degree[:per, None, :]
        n_pairs = 13
        gathered = gather(sent)
        crossed = swap(jnp.concatenate([part[:deep] for part in gathered[1:]]))
        crossed = [gathered[0][:deep]] + jnp.split(crossed, parts - 1)
        sent = apply_blocks(matrix, gathered, per, width, False)
        cross = sum(
            jnp.sum(blocks(out) * blocks(part), axis=(0, 2)) for out, part in zip(sent, crossed)
        )
        after = sent[0].shape[0] - deep - n_pairs - 1
        cross = lax.pad(
            cross[None], 0.0, ((deep + n_pairs, after, 0), (0, size - width, 0))
        )
        mine = collect([out + cross for out in sent])
        sums = mine[deep:]
        tail = sum(gather(sums))
        product = blocks(mine) + blocks(swap(mine[:deep]))
        qh = h + gains * (degree * h - product)
        g11, r1w1, r1w0, hh, hw1, hw0, w11, w10, w00, a_h0, a_10, a_00, hdh = (
            row_of(sums, n) for n in range(n_pairs)
        )
        a_hh = hh + gains * (hdh - 2.0 * row_of(tail, n_pairs))
        ratio0 = g11 / gamma0
        curve1 = r1w1 + 2.0 * ratio0 * r1w0 + ratio0 * ratio0 * delta0
        step1 = g11 / curve1
        e = step0 - step1
        f = -step1 * ratio0
        g22 = hh + 2.0 * (e * hw1 + f * hw0 + e * f * w10) + e * e * w11 + f * f * w00
        ratio1 = g22 / g11
        r2w1 = hw1 + e * w11 + f * w10
        r2w0 = hw0 + e * w10 + f * w00
        a_h1 = (hw1 - a_hh) / step0
        a_11 = (w11 - a_h1) / step0
        curve2 = a_hh + e * e * a_11 + f * f * a_00
        curve2 = curve2 + 2.0 * (e * a_h1 + f * a_h0 + e * f * a_10)
        curve2 = curve2 + 2.0 * ratio1 * (r2w1 + ratio0 * r2w0) + ratio1 * ratio1 * curve1
        step2 = g22 / curve2
        p1 = r1 + ratio0 * raw
        s1 = w1 + ratio0 * w0
        r2 = h + e * w1 + f * w0
        p2 = r2 + ratio1 * p1
        s2 = qh + e * (w1 - qh) / step0 + f * q0 + ratio1 * s1
        smoothed = step0 * raw + step1 * p1 + step2 * p2
        residual = r2 - step2 * s2

        def pick(field):
            return jnp.where(core == 0, field[:seg], field[seg:])

        return (pick(smoothed), pick(residual))

    return shards


def solution(mesh):
    placed = (
        P("row", "col", None, None, None),
        P("row", "col", None, None),
        P("row", "col"),
        P(),
        P(("row", "col"), None, None),
    )
    return jax.shard_map(
        build(mesh.shape["row"], mesh.shape["col"]),
        mesh=mesh,
        in_specs=placed,
        out_specs=(P(("row", "col"), None, None), P(("row", "col"), None, None)),
        check_vma=False,
    )
```

```python
import functools
import jax
import jax.numpy as jnp
from jax import lax
from jax.experimental import pallas as pl
from jax.experimental.pallas import tpu as pltpu
from jax.sharding import PartitionSpec as P

BF = jnp.bfloat16
F32 = jnp.float32
VMEM = pl.BlockSpec(memory_space=pltpu.VMEM)
SMEM = pl.BlockSpec(memory_space=pltpu.SMEM)
COPY = 8


def far_first(parts):
    return list(range(2, parts)) + [1]


def core_here():
    return lax.rem(lax.axis_index("col").astype(jnp.int32), 2)


def places_kernel(seg, index_ref, count_ref, raw_ref, out_ref, raw_out_ref):
    raw_out_ref[...] = raw_ref[...]
    row = lax.axis_index("row").astype(jnp.int32)
    col = lax.axis_index("col").astype(jnp.int32)
    line, core = lax.div(col, 2), lax.rem(col, 2)
    per = 2 * seg
    seg_bits, per_bits = seg.bit_length() - 1, per.bit_length() - 1
    u = index_ref[0, 0, 0:1]
    v = index_ref[0, 0, 1:2]
    out_ref[0:1] = ((u >> per_bits) ^ line) * per + (u & (per - 1))
    out_ref[1:2] = ((v >> seg_bits) ^ row) * per + core * seg + (v & (seg - 1))
    out_ref[2:3] = jnp.broadcast_to(count_ref[...], u.shape)


def find_places(block_index, block_count, raw):
    return pl.pallas_call(
        functools.partial(places_kernel, raw.shape[0]),
        in_specs=[VMEM, VMEM, VMEM],
        out_specs=[VMEM, VMEM],
        out_shape=[
            pltpu.VMEM((3, block_index.shape[3]), jnp.int32),
            pltpu.VMEM(raw.shape, F32),
        ],
    )(block_index, block_count, raw)


def split_kernel(own_places, other_places, own_hbm, other_in, own_out, other_out, own_in, sems):
    slots, size, _ = own_in.shape
    core = core_here()
    copies = []
    for chunk in range(slots // COPY):
        cut = pl.ds(chunk * COPY, COPY)
        copies.append(pltpu.make_async_copy(own_hbm.at[cut], own_in.at[cut], sems.at[chunk]))
    for copy in copies:
        copy.start()

    def write(turn):
        def sweep(places, source, target, chunk):
            live = chunk * COPY < places[2, 0]

            @pl.when(live)
            def _():
                for i in range(COPY):
                    slot = chunk * COPY + i
                    block = jnp.where(slot < places[2, 0], source[slot], 0.0)
                    block = block.T if turn else block
                    high = block.astype(BF)
                    target[slot, :size] = high
                    target[slot, size:] = (block - high.astype(F32)).astype(BF)

            @pl.when(jnp.logical_not(live))
            def _():
                target[pl.ds(chunk * COPY, COPY)] = jnp.zeros((COPY, 2 * size, size), BF)

        for chunk in range(slots // COPY):
            sweep(other_places, other_in, other_out, chunk)
        for chunk in range(slots // COPY):
            copies[chunk].wait()
            sweep(own_places, own_in, own_out, chunk)

    @pl.when(core == 0)
    def _():
        write(True)

    @pl.when(core != 0)
    def _():
        write(False)


def split_blocks(places, places_other, values, values_other):
    slots, size, _ = values.shape
    return pl.pallas_call(
        split_kernel,
        in_specs=[SMEM, SMEM, pl.BlockSpec(memory_space=pltpu.HBM), VMEM],
        out_specs=[VMEM, VMEM],
        out_shape=[pltpu.VMEM((slots, 2 * size, size), BF)] * 2,
        scratch_shapes=[
            pltpu.VMEM((slots, size, size), F32),
            pltpu.SemaphoreType.DMA((slots // COPY,)),
        ],
        compiler_params=pltpu.CompilerParams(vmem_limit_bytes=16 * 2**20),
        cost_estimate=pl.CostEstimate(
            flops=slots * size * size * 8, bytes_accessed=slots * size * size * 16, transcendentals=0
        ),
    )(
        places,
        places_other,
        pltpu.with_memory_space_constraint(values, pltpu.HBM),
        pltpu.with_memory_space_constraint(values_other, pltpu.VMEM),
    )


def apply_kernel(parts, per, width, with_degree, *refs):
    own_places, other_places, own_ref, other_ref = refs[:4]
    fields = [refs[4]] + [None] * (parts - 1)
    for part, ref in zip(far_first(parts), refs[5:]):
        fields[part] = ref
    outs = refs[4 + parts : 4 + 2 * parts]
    stack_ref, sum_ref = refs[4 + 2 * parts :]
    size = fields[0].shape[1]
    deep = per * width
    for part in range(parts):
        for j in range(per):
            x = fields[part][j * width : (j + 1) * width]
            high = x.astype(BF)
            low = (x - high.astype(F32)).astype(BF)
            f = part * per + j
            for half in range(2):
                cut = slice(half * size, (half + 1) * size)
                stack_ref[f, :width, cut] = high
                stack_ref[f, width : 2 * width, cut] = low
            if with_degree:
                stack_ref[f, 2 * width :, :] = jnp.ones((16, 2 * size), BF)
    sum_ref[...] = jnp.zeros_like(sum_ref)
    core = core_here()
    run = own_ref.shape[0]

    def sweep(values_ref, places):
        @pl.when(places[2, 0] > 0)
        def _():
            products = []
            for q in range(run):
                products.append(
                    jnp.dot(
                        stack_ref[places[1 - core, q]],
                        values_ref[q],
                        preferred_element_type=F32,
                    )
                )
            for q in range(run):
                to = places[core, q]
                whole = products[q]
                sum_ref[to, :width] += whole[:width] + whole[width : 2 * width]
                if with_degree:
                    sum_ref[to, width:] += whole[2 * width : 2 * width + 8]

    sweep(own_ref, own_places)
    sweep(other_ref, other_places)
    if not with_degree:
        aux = fields[0][deep:]
        for part in range(1, parts):
            aux = aux + fields[part][deep:]
    for part in range(parts):
        for j in range(per):
            outs[part][j * width : (j + 1) * width] = sum_ref[part * per + j, :width]
        if with_degree:
            outs[part][deep:] = jnp.zeros((8, size), F32)
            for j in range(per):
                row = deep + j
                outs[part][row : row + 1] = sum_ref[part * per + j, width : width + 1]
        else:
            outs[part][deep:] = aux


def apply_blocks(matrix, fields, per, width, with_degree):
    parts = len(fields)
    size = fields[0].shape[1]
    extra = 8 if with_degree else fields[0].shape[0] - per * width
    rows = 2 * width + (16 if with_degree else 0)
    sums = width + (8 if with_degree else 0)
    slots = matrix[2].shape[0]
    return pl.pallas_call(
        functools.partial(apply_kernel, parts, per, width, with_degree),
        in_specs=[SMEM] * 2 + [VMEM] * (2 + parts),
        out_specs=[VMEM] * parts,
        out_shape=[jax.ShapeDtypeStruct((per * width + extra, size), F32)] * parts,
        scratch_shapes=[
            pltpu.VMEM((parts * per, rows, 2 * size), BF),
            pltpu.VMEM((parts * per, sums, size), F32),
        ],
        compiler_params=pltpu.CompilerParams(vmem_limit_bytes=16 * 2**20),
        cost_estimate=pl.CostEstimate(
            flops=2 * slots * 4 * rows * size * size,
            bytes_accessed=4 * slots * size * size * 2,
            transcendentals=0,
        ),
    )(*matrix, fields[0], *(fields[part] for part in far_first(parts)))


def dot_rows(pairs, depth):
    width, size = pairs[0][0][0].shape
    lane = lax.broadcasted_iota(jnp.int32, (width, size), 1)
    table = jnp.zeros((width, size), F32)
    for n, (a, b) in enumerate(pairs):
        product = a[0] * b[0]
        for x, y in zip(a[1:], b[1:]):
            product = product + x * y
        table = jnp.where(lane == n, jnp.sum(product, axis=1, keepdims=True), table)
    square = jnp.concatenate([table, jnp.zeros((size - width, size), F32)], axis=0)
    return square.T[:depth]


def blocks_in(ref, per, width):
    return [ref[j * width : (j + 1) * width] for j in range(per)]


def put(ref, blocks):
    width = blocks[0].shape[0]
    for j, block in enumerate(blocks):
        ref[j * width : (j + 1) * width] = block


def first_update(per, mine, other, raw_ref, gain_ref, w0_out, degree_out, sent_out):
    width = raw_ref.shape[0] // per
    deep = per * width
    raw = blocks_in(raw_ref, per, width)
    degree = mine[deep:] + other[deep:]
    degree_out[...] = degree
    gain = gain_ref[...]
    w0 = []
    for j in range(per):
        cut = slice(j * width, (j + 1) * width)
        product = mine[cut] + other[cut]
        w0.append(raw[j] + gain * (degree[j : j + 1] * raw[j] - product))
    put(w0_out, w0)
    put(sent_out, w0)
    sent_out[deep:] = dot_rows([(raw, raw), (raw, w0)], sent_out.shape[0] - deep)


def second_update(per, mine, other, raw_ref, w0_ref, degree_ref, gain_ref, q0_out, r1_out, w1_out, sent_out):
    width = raw_ref.shape[0] // per
    deep = per * width
    raw, w0 = blocks_in(raw_ref, per, width), blocks_in(w0_ref, per, width)
    totals = jnp.concatenate(
        [
            0.5 * (mine[deep:] + other[deep:]),
            jnp.zeros((mine.shape[1] - mine.shape[0] + deep, mine.shape[1]), F32),
        ]
    ).T[:width]
    step0 = totals[:, 0:1] / totals[:, 1:2]
    degree, gain = degree_ref[...], gain_ref[...]
    q0, r1, w1, h, dh = [], [], [], [], []
    for j in range(per):
        cut = slice(j * width, (j + 1) * width)
        product = mine[cut] + other[cut]
        q0.append(w0[j] + gain * (degree[j : j + 1] * w0[j] - product))
        r1.append(raw[j] - step0 * w0[j])
        w1.append(w0[j] - step0 * q0[j])
        h.append(r1[j] - step0 * w1[j])
        dh.append(degree[j : j + 1] * h[j])
    put(q0_out, q0)
    put(r1_out, r1)
    put(w1_out, w1)
    put(sent_out, h)
    pairs = (
        (r1, r1),
        (r1, w1),
        (r1, w0),
        (h, h),
        (h, w1),
        (h, w0),
        (w1, w1),
        (w1, w0),
        (w0, w0),
        (h, q0),
        (w1, q0),
        (w0, q0),
        (dh, h),
    )
    sent_out[deep:] = dot_rows(pairs, sent_out.shape[0] - deep)


def cross_update(per, *refs, place):
    parts = (len(refs) - 2) // 2
    sent, (own_ref, crossed_ref), outs = refs[:parts], refs[parts : parts + 2], refs[parts + 2 :]
    size = own_ref.shape[1]
    deep = crossed_ref.shape[0] // (parts - 1)
    width = deep // per
    total = jnp.zeros((width, size), F32)
    for part in range(parts):
        for j in range(per):
            cut = slice(j * width, (j + 1) * width)
            if part == 0:
                field = own_ref[cut]
            else:
                first = (part - 1) * deep + j * width
                field = crossed_ref[first : first + width]
            total = total + sent[part][cut] * field
    lane = lax.broadcasted_iota(jnp.int32, (width, size), 1)
    table = jnp.where(lane == place, jnp.sum(total, axis=1, keepdims=True), 0.0)
    square = jnp.concatenate([table, jnp.zeros((size - width, size), F32)], axis=0).T
    for part in range(parts):
        outs[part][:deep] = sent[part][:deep]
        outs[part][deep:] = sent[part][deep:] + square[: sent[part].shape[0] - deep]


def update(kernel, per, shapes, *arrays):
    return pl.pallas_call(
        functools.partial(kernel, per),
        in_specs=[VMEM] * len(arrays),
        out_specs=[VMEM] * len(shapes),
        out_shape=[pltpu.VMEM(shape, F32) for shape in shapes],
        compiler_params=pltpu.CompilerParams(vmem_limit_bytes=16 * 2**20),
    )(*arrays)


def build(n_row, n_col):
    n_line = n_col // 2
    parts = max(n_row, n_line)

    def joint(array, offset, row_core, turn):
        pairs = []
        for r in range(n_row):
            for z in range(n_line):
                for k in range(2):
                    to_r, to_z = (r ^ offset, z) if k == row_core else (r, z ^ offset)
                    if to_r < n_row and to_z < n_line:
                        pairs.append((r * n_col + z * 2 + k, to_r * n_col + to_z * 2 + (k ^ turn)))
        return lax.ppermute(array, ("row", "col"), pairs)

    def swap(array):
        return lax.ppermute(array, "col", [(c, c ^ 1) for c in range(n_col)])

    def gather(field):
        return [field] + [joint(field, offset, 0, 0) for offset in range(1, parts)]

    def collect(sent):
        total = sent[0]
        for offset in reversed(far_first(parts)):
            total = total + joint(sent[offset], offset, 1, 1)
        return total

    def shards(block_values, block_index, block_count, strength, raw_scores):
        values = block_values[0, 0]
        core = core_here()
        seg = raw_scores.shape[0]
        per = 2 * seg
        raw_other = swap(raw_scores)
        places, raw_own = find_places(block_index, block_count, raw_scores)
        raw_other, raw_own, later_values = lax.optimization_barrier((raw_other, raw_own, values))
        values_other = swap(later_values)
        raw = jnp.where(
            core == 0,
            jnp.concatenate([raw_own, raw_other]),
            jnp.concatenate([raw_other, raw_own]),
        )
        places_other = swap(places)
        gains = strength[None, :, None]
        gathered = gather(raw.reshape(per * raw.shape[1], raw.shape[2]))
        values, values_other = lax.optimization_barrier((values, values_other))
        matrix = (places, places_other) + tuple(
            split_blocks(places, places_other, values, values_other)
        )

        width, size = raw.shape[1:]
        deep = per * width

        def blocks(array):
            return array[:deep].reshape(per, width, size)

        def row_of(aux, n):
            return aux[n, :width][None, :, None]

        flat = raw.reshape(deep, size)
        gain_rows = jnp.broadcast_to(strength[:, None], (width, size))
        deep_shape, aux_rows = (deep, size), 16

        mine = collect(apply_blocks(matrix, gathered, per, width, True))
        w0, degree, sent = update(
            first_update,
            per,
            (deep_shape, (8, size), (deep + aux_rows, size)),
            mine,
            swap(mine),
            flat,
            gain_rows,
        )

        mine = collect(apply_blocks(matrix, gather(sent), per, width, False))
        other = swap(mine)
        sums = 0.5 * (mine[deep:] + other[deep:])
        gamma0, delta0 = row_of(sums, 0), row_of(sums, 1)
        step0 = gamma0 / delta0
        q0, r1, w1, sent = update(
            second_update,
            per,
            (deep_shape,) * 3 + ((deep + aux_rows, size),),
            mine,
            other,
            flat,
            w0,
            degree,
            gain_rows,
        )
        h = blocks(sent)
        w0, q0, r1, w1 = blocks(w0), blocks(q0), blocks(r1), blocks(w1)
        degree = degree[:per, None, :]
        n_pairs = 13
        gathered = gather(sent)
        crossed = swap(jnp.concatenate([part[:deep] for part in gathered[1:]]))
        sent = apply_blocks(matrix, gathered, per, width, False)
        sent = update(
            functools.partial(cross_update, place=n_pairs),
            per,
            (sent[0].shape,) * parts,
            *sent,
            gathered[0],
            crossed,
        )
        mine = collect(sent)
        other = swap(mine)
        tail = 0.0
        for offset in reversed(far_first(parts)):
            tail = tail + joint(mine[deep:], offset, 1, 1)
        other, tail = lax.optimization_barrier((other, tail))
        tail = tail + other[deep:]
        sums = 0.5 * (mine[deep:] + other[deep:])
        product = blocks(mine) + blocks(other)
        qh = h + gains * (degree * h - product)
        g11, r1w1, r1w0, hh, hw1, hw0, w11, w10, w00, a_h0, a_10, a_00, hdh = (
            row_of(sums, n) for n in range(n_pairs)
        )
        a_hh = hh + gains * (hdh - 2.0 * row_of(tail, n_pairs))
        ratio0 = g11 / gamma0
        curve1 = r1w1 + 2.0 * ratio0 * r1w0 + ratio0 * ratio0 * delta0
        step1 = g11 / curve1
        e = step0 - step1
        f = -step1 * ratio0
        g22 = hh + 2.0 * (e * hw1 + f * hw0 + e * f * w10) + e * e * w11 + f * f * w00
        ratio1 = g22 / g11
        r2w1 = hw1 + e * w11 + f * w10
        r2w0 = hw0 + e * w10 + f * w00
        a_h1 = (hw1 - a_hh) / step0
        a_11 = (w11 - a_h1) / step0
        curve2 = a_hh + e * e * a_11 + f * f * a_00
        curve2 = curve2 + 2.0 * (e * a_h1 + f * a_h0 + e * f * a_10)
        curve2 = curve2 + 2.0 * ratio1 * (r2w1 + ratio0 * r2w0) + ratio1 * ratio1 * curve1
        step2 = g22 / curve2
        p1 = r1 + ratio0 * raw
        s1 = w1 + ratio0 * w0
        r2 = h + e * w1 + f * w0
        p2 = r2 + ratio1 * p1
        s2 = qh + e * (w1 - qh) / step0 + f * q0 + ratio1 * s1
        smoothed = step0 * raw + step1 * p1 + step2 * p2
        residual = r2 - step2 * s2

        def pick(field):
            return jnp.where(core == 0, field[:seg], field[seg:])

        return (pick(smoothed), pick(residual))

    return shards


def solution(mesh):
    placed = (
        P("row", "col", None, None, None),
        P("row", "col", None, None),
        P("row", "col"),
        P(),
        P(("row", "col"), None, None),
    )
    return jax.shard_map(
        build(mesh.shape["row"], mesh.shape["col"]),
        mesh=mesh,
        in_specs=placed,
        out_specs=(P(("row", "col"), None, None), P(("row", "col"), None, None)),
        check_vma=False,
    )
```

```python
import functools
import jax
import jax.numpy as jnp
from jax import lax
from jax.experimental import pallas as pl
from jax.experimental.pallas import tpu as pltpu
from jax.sharding import PartitionSpec as P

BF = jnp.bfloat16
F32 = jnp.float32
VMEM = pl.BlockSpec(memory_space=pltpu.VMEM)
SMEM = pl.BlockSpec(memory_space=pltpu.SMEM)
COPY = 8


def far_first(parts):
    return list(range(2, parts)) + [1]


def core_here():
    return lax.rem(lax.axis_index("col").astype(jnp.int32), 2)


def places_kernel(seg, index_ref, count_ref, raw_ref, out_ref, raw_out_ref):
    raw_out_ref[...] = raw_ref[...]
    row = lax.axis_index("row").astype(jnp.int32)
    col = lax.axis_index("col").astype(jnp.int32)
    line, core = lax.div(col, 2), lax.rem(col, 2)
    per = 2 * seg
    seg_bits, per_bits = seg.bit_length() - 1, per.bit_length() - 1
    u = index_ref[0, 0, 0:1]
    v = index_ref[0, 0, 1:2]
    out_ref[0:1] = ((u >> per_bits) ^ line) * per + (u & (per - 1))
    out_ref[1:2] = ((v >> seg_bits) ^ row) * per + core * seg + (v & (seg - 1))
    out_ref[2:3] = jnp.broadcast_to(count_ref[...], u.shape)


def find_places(block_index, block_count, raw):
    return pl.pallas_call(
        functools.partial(places_kernel, raw.shape[0]),
        in_specs=[VMEM, VMEM, VMEM],
        out_specs=[VMEM, VMEM],
        out_shape=[
            pltpu.VMEM((3, block_index.shape[3]), jnp.int32),
            pltpu.VMEM(raw.shape, F32),
        ],
    )(block_index, block_count, raw)


def split_kernel(own_vmem, other_vmem, own_hbm, other_in, own_out, other_out, own_places, other_places, own_in, sems):
    slots, size, _ = own_in.shape
    core = core_here()
    copies = []
    for chunk in range(slots // COPY):
        cut = pl.ds(chunk * COPY, COPY)
        copies.append(pltpu.make_async_copy(own_hbm.at[cut], own_in.at[cut], sems.at[chunk]))
    lists = [
        pltpu.make_async_copy(own_vmem, own_places, sems.at[slots // COPY]),
        pltpu.make_async_copy(other_vmem, other_places, sems.at[slots // COPY + 1]),
    ]
    for copy in lists + copies:
        copy.start()
    for copy in lists:
        copy.wait()

    def write(turn):
        def sweep(places, source, target, chunk):
            live = chunk * COPY < places[2, 0]

            @pl.when(live)
            def _():
                for i in range(COPY):
                    slot = chunk * COPY + i
                    block = jnp.where(slot < places[2, 0], source[slot], 0.0)
                    block = block.T if turn else block
                    high = block.astype(BF)
                    target[slot, :size] = high
                    target[slot, size:] = (block - high.astype(F32)).astype(BF)

            @pl.when(jnp.logical_not(live))
            def _():
                target[pl.ds(chunk * COPY, COPY)] = jnp.zeros((COPY, 2 * size, size), BF)

        for chunk in range(slots // COPY):
            sweep(other_places, other_in, other_out, chunk)
        for chunk in range(slots // COPY):
            copies[chunk].wait()
            sweep(own_places, own_in, own_out, chunk)

    @pl.when(core == 0)
    def _():
        write(True)

    @pl.when(core != 0)
    def _():
        write(False)


def split_blocks(places, places_other, values, values_other):
    slots, size, _ = values.shape
    return pl.pallas_call(
        split_kernel,
        in_specs=[VMEM, VMEM, pl.BlockSpec(memory_space=pltpu.HBM), VMEM],
        out_specs=[VMEM, VMEM, SMEM, SMEM],
        out_shape=[pltpu.VMEM((slots, 2 * size, size), BF)] * 2
        + [pltpu.SMEM(places.shape, jnp.int32)] * 2,
        scratch_shapes=[
            pltpu.VMEM((slots, size, size), F32),
            pltpu.SemaphoreType.DMA((slots // COPY + 2,)),
        ],
        compiler_params=pltpu.CompilerParams(vmem_limit_bytes=16 * 2**20),
        cost_estimate=pl.CostEstimate(
            flops=slots * size * size * 8, bytes_accessed=slots * size * size * 16, transcendentals=0
        ),
    )(
        places,
        places_other,
        pltpu.with_memory_space_constraint(values, pltpu.HBM),
        pltpu.with_memory_space_constraint(values_other, pltpu.VMEM),
    )


def apply_kernel(parts, per, width, with_degree, *refs):
    own_places, other_places, own_ref, other_ref = refs[:4]
    fields = [refs[4]] + [None] * (parts - 1)
    for part, ref in zip(far_first(parts), refs[5:]):
        fields[part] = ref
    outs = refs[4 + parts : 4 + 2 * parts]
    stack_ref, sum_ref = refs[4 + 2 * parts :]
    size = fields[0].shape[1]
    deep = per * width
    for part in range(parts):
        for j in range(per):
            x = fields[part][j * width : (j + 1) * width]
            high = x.astype(BF)
            low = (x - high.astype(F32)).astype(BF)
            f = part * per + j
            for half in range(2):
                cut = slice(half * size, (half + 1) * size)
                stack_ref[f, :width, cut] = high
                stack_ref[f, width : 2 * width, cut] = low
            if with_degree:
                stack_ref[f, 2 * width :, :] = jnp.ones((16, 2 * size), BF)
    sum_ref[...] = jnp.zeros_like(sum_ref)
    core = core_here()
    run = own_ref.shape[0]

    def sweep(values_ref, places):
        @pl.when(places[2, 0] > 0)
        def _():
            products = []
            for q in range(run):
                products.append(
                    jnp.dot(
                        stack_ref[places[1 - core, q]],
                        values_ref[q],
                        preferred_element_type=F32,
                    )
                )
            for q in range(run):
                to = places[core, q]
                whole = products[q]
                sum_ref[to, :width] += whole[:width] + whole[width : 2 * width]
                if with_degree:
                    sum_ref[to, width:] += whole[2 * width : 2 * width + 8]

    sweep(own_ref, own_places)
    sweep(other_ref, other_places)
    if not with_degree:
        aux = fields[0][deep:]
        for part in range(1, parts):
            aux = aux + fields[part][deep:]
    for part in range(parts):
        for j in range(per):
            outs[part][j * width : (j + 1) * width] = sum_ref[part * per + j, :width]
        if with_degree:
            outs[part][deep:] = jnp.zeros((8, size), F32)
            for j in range(per):
                row = deep + j
                outs[part][row : row + 1] = sum_ref[part * per + j, width : width + 1]
        else:
            outs[part][deep:] = aux


def apply_blocks(matrix, fields, per, width, with_degree):
    parts = len(fields)
    size = fields[0].shape[1]
    extra = 8 if with_degree else fields[0].shape[0] - per * width
    rows = 2 * width + (16 if with_degree else 0)
    sums = width + (8 if with_degree else 0)
    slots = matrix[2].shape[0]
    return pl.pallas_call(
        functools.partial(apply_kernel, parts, per, width, with_degree),
        in_specs=[SMEM] * 2 + [VMEM] * (2 + parts),
        out_specs=[VMEM] * parts,
        out_shape=[jax.ShapeDtypeStruct((per * width + extra, size), F32)] * parts,
        scratch_shapes=[
            pltpu.VMEM((parts * per, rows, 2 * size), BF),
            pltpu.VMEM((parts * per, sums, size), F32),
        ],
        compiler_params=pltpu.CompilerParams(vmem_limit_bytes=16 * 2**20),
        cost_estimate=pl.CostEstimate(
            flops=2 * slots * 4 * rows * size * size,
            bytes_accessed=4 * slots * size * size * 2,
            transcendentals=0,
        ),
    )(*matrix, fields[0], *(fields[part] for part in far_first(parts)))


def dot_rows(pairs, depth):
    width, size = pairs[0][0][0].shape
    lane = lax.broadcasted_iota(jnp.int32, (width, size), 1)
    table = jnp.zeros((width, size), F32)
    for n, (a, b) in enumerate(pairs):
        product = a[0] * b[0]
        for x, y in zip(a[1:], b[1:]):
            product = product + x * y
        table = jnp.where(lane == n, jnp.sum(product, axis=1, keepdims=True), table)
    square = jnp.concatenate([table, jnp.zeros((size - width, size), F32)], axis=0)
    return square.T[:depth]


def blocks_in(ref, per, width):
    return [ref[j * width : (j + 1) * width] for j in range(per)]


def put(ref, blocks):
    width = blocks[0].shape[0]
    for j, block in enumerate(blocks):
        ref[j * width : (j + 1) * width] = block


def first_update(per, mine, other, raw_ref, gain_ref, w0_out, degree_out, sent_out):
    width = raw_ref.shape[0] // per
    deep = per * width
    raw = blocks_in(raw_ref, per, width)
    degree = mine[deep:] + other[deep:]
    degree_out[...] = degree
    gain = gain_ref[...]
    w0 = []
    for j in range(per):
        cut = slice(j * width, (j + 1) * width)
        product = mine[cut] + other[cut]
        w0.append(raw[j] + gain * (degree[j : j + 1] * raw[j] - product))
    put(w0_out, w0)
    put(sent_out, w0)
    sent_out[deep:] = dot_rows([(raw, raw), (raw, w0)], sent_out.shape[0] - deep)


def second_update(per, mine, other, raw_ref, w0_ref, degree_ref, gain_ref, q0_out, r1_out, w1_out, sent_out):
    width = raw_ref.shape[0] // per
    deep = per * width
    raw, w0 = blocks_in(raw_ref, per, width), blocks_in(w0_ref, per, width)
    totals = jnp.concatenate(
        [
            0.5 * (mine[deep:] + other[deep:]),
            jnp.zeros((mine.shape[1] - mine.shape[0] + deep, mine.shape[1]), F32),
        ]
    ).T[:width]
    step0 = totals[:, 0:1] / totals[:, 1:2]
    degree, gain = degree_ref[...], gain_ref[...]
    q0, r1, w1, h, dh = [], [], [], [], []
    for j in range(per):
        cut = slice(j * width, (j + 1) * width)
        product = mine[cut] + other[cut]
        q0.append(w0[j] + gain * (degree[j : j + 1] * w0[j] - product))
        r1.append(raw[j] - step0 * w0[j])
        w1.append(w0[j] - step0 * q0[j])
        h.append(r1[j] - step0 * w1[j])
        dh.append(degree[j : j + 1] * h[j])
    put(q0_out, q0)
    put(r1_out, r1)
    put(w1_out, w1)
    put(sent_out, h)
    pairs = (
        (r1, r1),
        (r1, w1),
        (r1, w0),
        (h, h),
        (h, w1),
        (h, w0),
        (w1, w1),
        (w1, w0),
        (w0, w0),
        (h, q0),
        (w1, q0),
        (w0, q0),
        (dh, h),
    )
    sent_out[deep:] = dot_rows(pairs, sent_out.shape[0] - deep)


def cross_update(per, *refs, place):
    parts = (len(refs) - 2) // 2
    sent, (own_ref, crossed_ref), outs = refs[:parts], refs[parts : parts + 2], refs[parts + 2 :]
    size = own_ref.shape[1]
    deep = crossed_ref.shape[0] // (parts - 1)
    width = deep // per
    total = jnp.zeros((width, size), F32)
    for part in range(parts):
        for j in range(per):
            cut = slice(j * width, (j + 1) * width)
            if part == 0:
                field = own_ref[cut]
            else:
                first = (part - 1) * deep + j * width
                field = crossed_ref[first : first + width]
            total = total + sent[part][cut] * field
    lane = lax.broadcasted_iota(jnp.int32, (width, size), 1)
    table = jnp.where(lane == place, jnp.sum(total, axis=1, keepdims=True), 0.0)
    square = jnp.concatenate([table, jnp.zeros((size - width, size), F32)], axis=0).T
    for part in range(parts):
        outs[part][:deep] = sent[part][:deep]
        outs[part][deep:] = sent[part][deep:] + square[: sent[part].shape[0] - deep]


def update(kernel, per, shapes, *arrays):
    return pl.pallas_call(
        functools.partial(kernel, per),
        in_specs=[VMEM] * len(arrays),
        out_specs=[VMEM] * len(shapes),
        out_shape=[pltpu.VMEM(shape, F32) for shape in shapes],
        compiler_params=pltpu.CompilerParams(vmem_limit_bytes=16 * 2**20),
    )(*arrays)


def build(n_row, n_col):
    n_line = n_col // 2
    parts = max(n_row, n_line)

    def joint(array, offset, row_core, turn):
        pairs = []
        for r in range(n_row):
            for z in range(n_line):
                for k in range(2):
                    to_r, to_z = (r ^ offset, z) if k == row_core else (r, z ^ offset)
                    if to_r < n_row and to_z < n_line:
                        pairs.append((r * n_col + z * 2 + k, to_r * n_col + to_z * 2 + (k ^ turn)))
        return lax.ppermute(array, ("row", "col"), pairs)

    def swap(array):
        return lax.ppermute(array, "col", [(c, c ^ 1) for c in range(n_col)])

    def gather(field):
        return [field] + [joint(field, offset, 0, 0) for offset in range(1, parts)]

    def collect(sent):
        total = sent[0]
        for offset in reversed(far_first(parts)):
            total = total + joint(sent[offset], offset, 1, 1)
        return total

    def shards(block_values, block_index, block_count, strength, raw_scores):
        values = block_values[0, 0]
        core = core_here()
        seg = raw_scores.shape[0]
        per = 2 * seg
        raw_other = swap(raw_scores)
        places, raw_own = find_places(block_index, block_count, raw_scores)
        raw_other, raw_own, later_values = lax.optimization_barrier((raw_other, raw_own, values))
        values_other = swap(later_values)
        raw = jnp.where(
            core == 0,
            jnp.concatenate([raw_own, raw_other]),
            jnp.concatenate([raw_other, raw_own]),
        )
        places_other = swap(places)
        gains = strength[None, :, None]
        gathered = gather(raw.reshape(per * raw.shape[1], raw.shape[2]))
        values, values_other = lax.optimization_barrier((values, values_other))
        own, other, places, places_other = split_blocks(places, places_other, values, values_other)
        matrix = (places, places_other, own, other)

        width, size = raw.shape[1:]
        deep = per * width

        def blocks(array):
            return array[:deep].reshape(per, width, size)

        def row_of(aux, n):
            return aux[n, :width][None, :, None]

        flat = raw.reshape(deep, size)
        gain_rows = jnp.broadcast_to(strength[:, None], (width, size))
        deep_shape, aux_rows = (deep, size), 16

        mine = collect(apply_blocks(matrix, gathered, per, width, True))
        w0, degree, sent = update(
            first_update,
            per,
            (deep_shape, (8, size), (deep + aux_rows, size)),
            mine,
            swap(mine),
            flat,
            gain_rows,
        )

        mine = collect(apply_blocks(matrix, gather(sent), per, width, False))
        other = swap(mine)
        sums = 0.5 * (mine[deep:] + other[deep:])
        gamma0, delta0 = row_of(sums, 0), row_of(sums, 1)
        step0 = gamma0 / delta0
        q0, r1, w1, sent = update(
            second_update,
            per,
            (deep_shape,) * 3 + ((deep + aux_rows, size),),
            mine,
            other,
            flat,
            w0,
            degree,
            gain_rows,
        )
        h = blocks(sent)
        w0, q0, r1, w1 = blocks(w0), blocks(q0), blocks(r1), blocks(w1)
        degree = degree[:per, None, :]
        n_pairs = 13
        gathered = gather(sent)
        crossed = swap(jnp.concatenate([part[:deep] for part in gathered[1:]]))
        sent = apply_blocks(matrix, gathered, per, width, False)
        sent = update(
            functools.partial(cross_update, place=n_pairs),
            per,
            (sent[0].shape,) * parts,
            *sent,
            gathered[0],
            crossed,
        )
        mine = collect(sent)
        other = swap(mine)
        tail = 0.0
        for offset in reversed(range(1, parts)):
            tail = tail + joint(mine[deep:], offset, 1, 1)
        other, tail = lax.optimization_barrier((other, tail))
        tail = tail + other[deep:]
        sums = 0.5 * (mine[deep:] + other[deep:])
        product = blocks(mine) + blocks(other)
        qh = h + gains * (degree * h - product)
        g11, r1w1, r1w0, hh, hw1, hw0, w11, w10, w00, a_h0, a_10, a_00, hdh = (
            row_of(sums, n) for n in range(n_pairs)
        )
        a_hh = hh + gains * (hdh - 2.0 * row_of(tail, n_pairs))
        ratio0 = g11 / gamma0
        curve1 = r1w1 + 2.0 * ratio0 * r1w0 + ratio0 * ratio0 * delta0
        step1 = g11 / curve1
        e = step0 - step1
        f = -step1 * ratio0
        g22 = hh + 2.0 * (e * hw1 + f * hw0 + e * f * w10) + e * e * w11 + f * f * w00
        ratio1 = g22 / g11
        r2w1 = hw1 + e * w11 + f * w10
        r2w0 = hw0 + e * w10 + f * w00
        a_h1 = (hw1 - a_hh) / step0
        a_11 = (w11 - a_h1) / step0
        curve2 = a_hh + e * e * a_11 + f * f * a_00
        curve2 = curve2 + 2.0 * (e * a_h1 + f * a_h0 + e * f * a_10)
        curve2 = curve2 + 2.0 * ratio1 * (r2w1 + ratio0 * r2w0) + ratio1 * ratio1 * curve1
        step2 = g22 / curve2
        p1 = r1 + ratio0 * raw
        s1 = w1 + ratio0 * w0
        r2 = h + e * w1 + f * w0
        p2 = r2 + ratio1 * p1
        s2 = qh + e * (w1 - qh) / step0 + f * q0 + ratio1 * s1
        smoothed = step0 * raw + step1 * p1 + step2 * p2
        residual = r2 - step2 * s2

        def pick(field):
            return jnp.where(core == 0, field[:seg], field[seg:])

        return (pick(smoothed), pick(residual))

    return shards


def solution(mesh):
    placed = (
        P("row", "col", None, None, None),
        P("row", "col", None, None),
        P("row", "col"),
        P(),
        P(("row", "col"), None, None),
    )
    return jax.shard_map(
        build(mesh.shape["row"], mesh.shape["col"]),
        mesh=mesh,
        in_specs=placed,
        out_specs=(P(("row", "col"), None, None), P(("row", "col"), None, None)),
        check_vma=False,
    )
```

```python
import functools
import jax
import jax.numpy as jnp
from jax import lax
from jax.experimental import pallas as pl
from jax.experimental.pallas import tpu as pltpu
from jax.sharding import PartitionSpec as P

BF = jnp.bfloat16
F32 = jnp.float32
VMEM = pl.BlockSpec(memory_space=pltpu.VMEM)
SMEM = pl.BlockSpec(memory_space=pltpu.SMEM)
COPY = 8


def far_first(parts):
    return list(range(2, parts)) + [1]


def core_here():
    return lax.rem(lax.axis_index("col").astype(jnp.int32), 2)


def places_kernel(seg, index_ref, count_ref, raw_ref, out_ref, raw_out_ref):
    raw_out_ref[...] = raw_ref[...]
    row = lax.axis_index("row").astype(jnp.int32)
    col = lax.axis_index("col").astype(jnp.int32)
    line, core = lax.div(col, 2), lax.rem(col, 2)
    per = 2 * seg
    seg_bits, per_bits = seg.bit_length() - 1, per.bit_length() - 1
    u = index_ref[0, 0, 0:1]
    v = index_ref[0, 0, 1:2]
    out_ref[0:1] = ((u >> per_bits) ^ line) * per + (u & (per - 1))
    out_ref[1:2] = ((v >> seg_bits) ^ row) * per + core * seg + (v & (seg - 1))
    out_ref[2:3] = jnp.broadcast_to(count_ref[...], u.shape)


def find_places(block_index, block_count, raw):
    return pl.pallas_call(
        functools.partial(places_kernel, raw.shape[0]),
        in_specs=[VMEM, VMEM, VMEM],
        out_specs=[VMEM, VMEM],
        out_shape=[
            pltpu.VMEM((3, block_index.shape[3]), jnp.int32),
            pltpu.VMEM(raw.shape, F32),
        ],
    )(block_index, block_count, raw)


def split_kernel(own_vmem, other_vmem, own_hbm, other_in, own_out, other_out, own_places, other_places, own_in, sems):
    slots, size, _ = own_in.shape
    core = core_here()
    copies = []
    for chunk in range(slots // COPY):
        cut = pl.ds(chunk * COPY, COPY)
        copies.append(pltpu.make_async_copy(own_hbm.at[cut], own_in.at[cut], sems.at[chunk]))
    lists = [
        pltpu.make_async_copy(own_vmem, own_places, sems.at[slots // COPY]),
        pltpu.make_async_copy(other_vmem, other_places, sems.at[slots // COPY + 1]),
    ]
    for copy in lists + copies:
        copy.start()
    for copy in lists:
        copy.wait()

    def write(turn):
        def sweep(places, source, target, chunk):
            live = chunk * COPY < places[2, 0]

            @pl.when(live)
            def _():
                for i in range(COPY):
                    slot = chunk * COPY + i
                    block = jnp.where(slot < places[2, 0], source[slot], 0.0)
                    block = block.T if turn else block
                    high = block.astype(BF)
                    target[slot, :size] = high
                    target[slot, size:] = (block - high.astype(F32)).astype(BF)

            @pl.when(jnp.logical_not(live))
            def _():
                target[pl.ds(chunk * COPY, COPY)] = jnp.zeros((COPY, 2 * size, size), BF)

        for chunk in range(slots // COPY):
            sweep(other_places, other_in, other_out, chunk)
        for chunk in range(slots // COPY):
            copies[chunk].wait()
            sweep(own_places, own_in, own_out, chunk)

    @pl.when(core == 0)
    def _():
        write(True)

    @pl.when(core != 0)
    def _():
        write(False)


def split_blocks(places, places_other, values, values_other):
    slots, size, _ = values.shape
    return pl.pallas_call(
        split_kernel,
        in_specs=[VMEM, VMEM, pl.BlockSpec(memory_space=pltpu.HBM), VMEM],
        out_specs=[VMEM, VMEM, SMEM, SMEM],
        out_shape=[pltpu.VMEM((slots, 2 * size, size), BF)] * 2
        + [pltpu.SMEM(places.shape, jnp.int32)] * 2,
        scratch_shapes=[
            pltpu.VMEM((slots, size, size), F32),
            pltpu.SemaphoreType.DMA((slots // COPY + 2,)),
        ],
        compiler_params=pltpu.CompilerParams(vmem_limit_bytes=16 * 2**20),
        cost_estimate=pl.CostEstimate(
            flops=slots * size * size * 8, bytes_accessed=slots * size * size * 16, transcendentals=0
        ),
    )(
        places,
        places_other,
        pltpu.with_memory_space_constraint(values, pltpu.HBM),
        pltpu.with_memory_space_constraint(values_other, pltpu.VMEM),
    )


def apply_kernel(parts, per, width, with_degree, *refs):
    own_places, other_places, own_ref, other_ref = refs[:4]
    fields = [refs[4]] + [None] * (parts - 1)
    for part, ref in zip(far_first(parts), refs[5:]):
        fields[part] = ref
    outs = refs[4 + parts : 4 + 2 * parts]
    stack_ref, sum_ref = refs[4 + 2 * parts :]
    size = fields[0].shape[1]
    deep = per * width
    for part in range(parts):
        for j in range(per):
            x = fields[part][j * width : (j + 1) * width]
            high = x.astype(BF)
            low = (x - high.astype(F32)).astype(BF)
            f = part * per + j
            for half in range(2):
                cut = slice(half * size, (half + 1) * size)
                stack_ref[f, :width, cut] = high
                stack_ref[f, width : 2 * width, cut] = low
            if with_degree:
                stack_ref[f, 2 * width :, :] = jnp.ones((16, 2 * size), BF)
    sum_ref[...] = jnp.zeros_like(sum_ref)
    core = core_here()
    run = own_ref.shape[0]

    def sweep(values_ref, places):
        @pl.when(places[2, 0] > 0)
        def _():
            products = []
            for q in range(run):
                products.append(
                    jnp.dot(
                        stack_ref[places[1 - core, q]],
                        values_ref[q],
                        preferred_element_type=F32,
                    )
                )
            for q in range(run):
                to = places[core, q]
                whole = products[q]
                sum_ref[to, :width] += whole[:width] + whole[width : 2 * width]
                if with_degree:
                    sum_ref[to, width:] += whole[2 * width : 2 * width + 8]

    sweep(own_ref, own_places)
    sweep(other_ref, other_places)
    if not with_degree:
        aux = fields[0][deep:]
        for part in range(1, parts):
            aux = aux + fields[part][deep:]
    for part in range(parts):
        for j in range(per):
            outs[part][j * width : (j + 1) * width] = sum_ref[part * per + j, :width]
        if with_degree:
            outs[part][deep:] = jnp.zeros((8, size), F32)
            for j in range(per):
                row = deep + j
                outs[part][row : row + 1] = sum_ref[part * per + j, width : width + 1]
        else:
            outs[part][deep:] = aux


def apply_blocks(matrix, fields, per, width, with_degree):
    parts = len(fields)
    size = fields[0].shape[1]
    extra = 8 if with_degree else fields[0].shape[0] - per * width
    rows = 2 * width + (16 if with_degree else 0)
    sums = width + (8 if with_degree else 0)
    slots = matrix[2].shape[0]
    return pl.pallas_call(
        functools.partial(apply_kernel, parts, per, width, with_degree),
        in_specs=[SMEM] * 2 + [VMEM] * (2 + parts),
        out_specs=[VMEM] * parts,
        out_shape=[jax.ShapeDtypeStruct((per * width + extra, size), F32)] * parts,
        scratch_shapes=[
            pltpu.VMEM((parts * per, rows, 2 * size), BF),
            pltpu.VMEM((parts * per, sums, size), F32),
        ],
        compiler_params=pltpu.CompilerParams(vmem_limit_bytes=16 * 2**20),
        cost_estimate=pl.CostEstimate(
            flops=2 * slots * 4 * rows * size * size,
            bytes_accessed=4 * slots * size * size * 2,
            transcendentals=0,
        ),
    )(*matrix, fields[0], *(fields[part] for part in far_first(parts)))


def dot_rows(pairs, depth):
    width, size = pairs[0][0][0].shape
    lane = lax.broadcasted_iota(jnp.int32, (width, size), 1)
    table = jnp.zeros((width, size), F32)
    for n, (a, b) in enumerate(pairs):
        product = a[0] * b[0]
        for x, y in zip(a[1:], b[1:]):
            product = product + x * y
        table = jnp.where(lane == n, jnp.sum(product, axis=1, keepdims=True), table)
    square = jnp.concatenate([table, jnp.zeros((size - width, size), F32)], axis=0)
    return square.T[:depth]


def blocks_in(ref, per, width):
    return [ref[j * width : (j + 1) * width] for j in range(per)]


def put(ref, blocks):
    width = blocks[0].shape[0]
    for j, block in enumerate(blocks):
        ref[j * width : (j + 1) * width] = block


def first_update(per, mine, other, raw_ref, gain_ref, w0_out, degree_out, sent_out):
    width = raw_ref.shape[0] // per
    deep = per * width
    raw = blocks_in(raw_ref, per, width)
    degree = mine[deep:] + other[deep:]
    degree_out[...] = degree
    gain = gain_ref[...]
    w0 = []
    for j in range(per):
        cut = slice(j * width, (j + 1) * width)
        product = mine[cut] + other[cut]
        w0.append(raw[j] + gain * (degree[j : j + 1] * raw[j] - product))
    put(w0_out, w0)
    put(sent_out, w0)
    sent_out[deep:] = dot_rows([(raw, raw), (raw, w0)], sent_out.shape[0] - deep)


def second_update(per, mine, other, raw_ref, w0_ref, degree_ref, gain_ref, q0_out, r1_out, w1_out, sent_out):
    width = raw_ref.shape[0] // per
    deep = per * width
    raw, w0 = blocks_in(raw_ref, per, width), blocks_in(w0_ref, per, width)
    totals = jnp.concatenate(
        [
            0.5 * (mine[deep:] + other[deep:]),
            jnp.zeros((mine.shape[1] - mine.shape[0] + deep, mine.shape[1]), F32),
        ]
    ).T[:width]
    step0 = totals[:, 0:1] / totals[:, 1:2]
    degree, gain = degree_ref[...], gain_ref[...]
    q0, r1, w1, h, dh = [], [], [], [], []
    for j in range(per):
        cut = slice(j * width, (j + 1) * width)
        product = mine[cut] + other[cut]
        q0.append(w0[j] + gain * (degree[j : j + 1] * w0[j] - product))
        r1.append(raw[j] - step0 * w0[j])
        w1.append(w0[j] - step0 * q0[j])
        h.append(r1[j] - step0 * w1[j])
        dh.append(degree[j : j + 1] * h[j])
    put(q0_out, q0)
    put(r1_out, r1)
    put(w1_out, w1)
    put(sent_out, h)
    pairs = (
        (r1, r1),
        (r1, w1),
        (r1, w0),
        (h, h),
        (h, w1),
        (h, w0),
        (w1, w1),
        (w1, w0),
        (w0, w0),
        (h, q0),
        (w1, q0),
        (w0, q0),
        (dh, h),
    )
    sent_out[deep:] = dot_rows(pairs, sent_out.shape[0] - deep)


def cross_update(per, *refs, place):
    parts = (len(refs) - 2) // 2
    sent, (own_ref, crossed_ref), outs = refs[:parts], refs[parts : parts + 2], refs[parts + 2 :]
    size = own_ref.shape[1]
    deep = crossed_ref.shape[0] // (parts - 1)
    width = deep // per
    total = jnp.zeros((width, size), F32)
    for part in range(parts):
        for j in range(per):
            cut = slice(j * width, (j + 1) * width)
            if part == 0:
                field = own_ref[cut]
            else:
                first = (part - 1) * deep + j * width
                field = crossed_ref[first : first + width]
            total = total + sent[part][cut] * field
    lane = lax.broadcasted_iota(jnp.int32, (width, size), 1)
    table = jnp.where(lane == place, jnp.sum(total, axis=1, keepdims=True), 0.0)
    square = jnp.concatenate([table, jnp.zeros((size - width, size), F32)], axis=0).T
    for part in range(parts):
        outs[part][:deep] = sent[part][:deep]
        outs[part][deep:] = sent[part][deep:] + square[: sent[part].shape[0] - deep]


def update(kernel, per, shapes, *arrays):
    return pl.pallas_call(
        functools.partial(kernel, per),
        in_specs=[VMEM] * len(arrays),
        out_specs=[VMEM] * len(shapes),
        out_shape=[pltpu.VMEM(shape, F32) for shape in shapes],
        compiler_params=pltpu.CompilerParams(vmem_limit_bytes=16 * 2**20),
    )(*arrays)


def build(n_row, n_col):
    n_line = n_col // 2
    parts = max(n_row, n_line)

    def joint(array, offset, row_core, turn):
        pairs = []
        for r in range(n_row):
            for z in range(n_line):
                for k in range(2):
                    to_r, to_z = (r ^ offset, z) if k == row_core else (r, z ^ offset)
                    if to_r < n_row and to_z < n_line:
                        pairs.append((r * n_col + z * 2 + k, to_r * n_col + to_z * 2 + (k ^ turn)))
        return lax.ppermute(array, ("row", "col"), pairs)

    def swap(array):
        return lax.ppermute(array, "col", [(c, c ^ 1) for c in range(n_col)])

    def gather(field):
        return [field] + [joint(field, offset, 0, 0) for offset in range(1, parts)]

    def collect(sent):
        total = sent[0]
        for offset in reversed(far_first(parts)):
            total = total + joint(sent[offset], offset, 1, 1)
        return total

    def shards(block_values, block_index, block_count, strength, raw_scores):
        values = block_values[0, 0]
        core = core_here()
        seg = raw_scores.shape[0]
        per = 2 * seg
        raw_other = swap(raw_scores)
        places, raw_own = find_places(block_index, block_count, raw_scores)
        raw_other, raw_own, later_values = lax.optimization_barrier((raw_other, raw_own, values))
        values_other = swap(later_values)
        raw = jnp.where(
            core == 0,
            jnp.concatenate([raw_own, raw_other]),
            jnp.concatenate([raw_other, raw_own]),
        )
        places_other = swap(places)
        gains = strength[None, :, None]
        gathered = gather(raw.reshape(per * raw.shape[1], raw.shape[2]))
        values, values_other = lax.optimization_barrier((values, values_other))
        own, other, places, places_other = split_blocks(places, places_other, values, values_other)
        matrix = (places, places_other, own, other)

        width, size = raw.shape[1:]
        deep = per * width

        def blocks(array):
            return array[:deep].reshape(per, width, size)

        def row_of(aux, n):
            return aux[n, :width][None, :, None]

        flat = raw.reshape(deep, size)
        gain_rows = jnp.broadcast_to(strength[:, None], (width, size))
        deep_shape, aux_rows = (deep, size), 16

        mine = collect(apply_blocks(matrix, gathered, per, width, True))
        w0, degree, sent = update(
            first_update,
            per,
            (deep_shape, (8, size), (deep + aux_rows, size)),
            mine,
            swap(mine),
            flat,
            gain_rows,
        )

        mine = collect(apply_blocks(matrix, gather(sent), per, width, False))
        other = swap(mine)
        sums = 0.5 * (mine[deep:] + other[deep:])
        gamma0, delta0 = row_of(sums, 0), row_of(sums, 1)
        step0 = gamma0 / delta0
        q0, r1, w1, sent = update(
            second_update,
            per,
            (deep_shape,) * 3 + ((deep + aux_rows, size),),
            mine,
            other,
            flat,
            w0,
            degree,
            gain_rows,
        )
        h = blocks(sent)
        w0, q0, r1, w1 = blocks(w0), blocks(q0), blocks(r1), blocks(w1)
        degree = degree[:per, None, :]
        n_pairs = 13
        gathered = gather(sent)
        crossed = swap(jnp.concatenate([part[:deep] for part in gathered[1:]]))
        sent = apply_blocks(matrix, gathered, per, width, False)
        sent = update(
            functools.partial(cross_update, place=n_pairs),
            per,
            (sent[0].shape,) * parts,
            *sent,
            gathered[0],
            crossed,
        )
        mine = collect(sent)
        other = swap(mine)
        tail = 0.0
        for offset in reversed(range(1, parts)):
            tail = tail + joint(mine[deep:], offset, 1, 1)
        other, tail = lax.optimization_barrier((other, tail))
        tail = tail + other[deep:]
        sums = 0.5 * (mine[deep:] + other[deep:])
        product = blocks(mine) + blocks(other)
        qh = h + gains * (degree * h - product)
        g11, r1w1, r1w0, hh, hw1, hw0, w11, w10, w00, a_h0, a_10, a_00, hdh = (
            row_of(sums, n) for n in range(n_pairs)
        )
        a_hh = hh + gains * (hdh - 2.0 * row_of(tail, n_pairs))
        ratio0 = g11 / gamma0
        curve1 = r1w1 + 2.0 * ratio0 * r1w0 + ratio0 * ratio0 * delta0
        step1 = g11 / curve1
        e = step0 - step1
        f = -step1 * ratio0
        g22 = hh + 2.0 * (e * hw1 + f * hw0 + e * f * w10) + e * e * w11 + f * f * w00
        ratio1 = g22 / g11
        r2w1 = hw1 + e * w11 + f * w10
        r2w0 = hw0 + e * w10 + f * w00
        a_h1 = (hw1 - a_hh) / step0
        a_11 = (w11 - a_h1) / step0
        curve2 = a_hh + e * e * a_11 + f * f * a_00
        curve2 = curve2 + 2.0 * (e * a_h1 + f * a_h0 + e * f * a_10)
        curve2 = curve2 + 2.0 * ratio1 * (r2w1 + ratio0 * r2w0) + ratio1 * ratio1 * curve1
        step2 = g22 / curve2

        def pick(field):
            return jnp.where(core == 0, field[:seg], field[seg:])

        raw, r1, w0, w1, h, q0, qh = (pick(field) for field in (raw, r1, w0, w1, h, q0, qh))
        p1 = r1 + ratio0 * raw
        s1 = w1 + ratio0 * w0
        r2 = h + e * w1 + f * w0
        p2 = r2 + ratio1 * p1
        s2 = qh + e * (w1 - qh) / step0 + f * q0 + ratio1 * s1
        smoothed = step0 * raw + step1 * p1 + step2 * p2
        residual = r2 - step2 * s2

        return (smoothed, residual)

    return shards


def solution(mesh):
    placed = (
        P("row", "col", None, None, None),
        P("row", "col", None, None),
        P("row", "col"),
        P(),
        P(("row", "col"), None, None),
    )
    return jax.shard_map(
        build(mesh.shape["row"], mesh.shape["col"]),
        mesh=mesh,
        in_specs=placed,
        out_specs=(P(("row", "col"), None, None), P(("row", "col"), None, None)),
        check_vma=False,
    )
```
